512 devices in a mesh: lon: 32 (over x_lo, z), lat: 8 (over y, core), mem: 2 (over x_hi).
Axes of the slice: x: 4 (x_hi: 2, x_lo: 2; x = x_hi * 2 + x_lo), y: 4, z: 16, core: 2. Of those that a mesh axis runs over, the one named last changes fastest.
Arguments:
- states: bfloat16 [2, 4, 48, 73728], P('mem', None, 'lat', 'lon'), may hold values from -6 to 6
- cotangent: bfloat16 [2, 4, 48, 73728], P('mem', None, 'lat', 'lon'), may hold values from -6 to 6
- region: int32 [48, 4], P('lat'), may hold values from 0 to 2
- pos_index: int32 [144, 144], replicated, may hold values from 0 to 3311
- w_qkv: bfloat16 [192, 576], replicated, may hold values from -0.4375 to 0.4375
- w_proj: bfloat16 [192, 192], replicated, may hold values from -0.4375 to 0.4375
- w_up: bfloat16 [192, 768], replicated, may hold values from -0.4375 to 0.4375
- w_down: bfloat16 [768, 192], replicated, may hold values from -0.21875 to 0.21875
- gains: float32 [2, 192], replicated, may hold values from 0.1 to 1.9
- earth_bias: float32 [8, 6, 3312], P('lat'), may hold values from -4 to 4
Outputs:
- grad_states: bfloat16 [2, 4, 48, 73728], P('mem', None, 'lat', 'lon')
- grad_qkv: float32 [192, 576], replicated
- grad_proj: float32 [192, 192], replicated
- grad_up: float32 [192, 768], replicated
- grad_down: float32 [768, 192], replicated
- grad_gains: float32 [2, 192], replicated
- grad_bias: float32 [8, 6, 3312], P('lat')
The draws below stay inside these ranges and needn't reach their ends.
All inputs are finite; a program needn't handle non-finite values.
Results may differ from the reference program's by a relative error of at most 0.02.
Values may be sent and summed in bfloat16 or wider, within the bound.
No kernel may reach another device: no remote copies, remote signals or barrier semaphores. Data moves between devices by JAX's collectives and lax.ppermute only.
A program may use at most 64 MiB of HBM per device.

```python
import jax
import jax.numpy as jnp
from jax import lax

C = 192
HEADS = 6
FF = 768
WIN_PL = 2
WIN_LAT = 6
WIN_LON = 12
PL = 4
WIN = 144
BIAS_POS = 3312
MEMBERS = 2
NLAT = 48
NLON = 384
NLATW = 8


def with_ends(result, stream_key, least, largest):
    longest = result.shape.index(max(result.shape))
    spots = []
    for shift in (0, 1):
        where = [jax.random.randint(jax.random.fold_in(stream_key, axis), (), 0, length) for axis, length in enumerate(result.shape)]
        where[longest] = (where[longest] + shift) % result.shape[longest]
        spots.append(tuple(where))
    return result.at[spots[0]].set(least).at[spots[1]].set(largest)


def block_levels(own_key, shape, split, low, high):
    factor_of = 1.0
    for axis_at, parts in split:
        heights = jax.random.uniform(jax.random.fold_in(jax.random.fold_in(own_key, 6), axis_at), (parts,), jnp.float32, low / len(split), high / len(split))
        factor_of = factor_of * jnp.repeat(jnp.exp(heights), shape[axis_at] // parts).reshape((-1,) + (1,) * (len(shape) - 1 - axis_at))
    return factor_of


def noise(own_key, shape, scale, bound, pieces=(), kind=jnp.bfloat16):
    level = block_levels(own_key, shape, pieces, -0.22, 0.18) if pieces else 1.0
    drawn = jax.random.normal(own_key, shape, jnp.float32) * scale * level
    return jnp.minimum(jnp.maximum(drawn, -bound), bound).astype(kind)


def setup_inputs(seed: int = 0) -> dict:
    splits = jax.random.split(jax.random.key(seed), 11)
    return {
        "states": noise(splits[0], (MEMBERS, PL, NLAT, NLON * C), 1.0, 6.0, ((0, 2), (2, 8), (3, 32))),
        "cotangent": noise(splits[1], (MEMBERS, PL, NLAT, NLON * C), 1.0, 6.0, ((0, 2), (2, 8), (3, 32))),
        "region": with_ends(jax.random.randint(splits[2], (NLAT, PL), 0, 3), jax.random.fold_in(splits[2], 1), 0, 2).astype(jnp.int32),
        "pos_index": with_ends(jax.random.randint(splits[3], (WIN, WIN), 0, BIAS_POS), jax.random.fold_in(splits[3], 1), 0, BIAS_POS - 1).astype(jnp.int32),
        "w_qkv": noise(splits[4], (C, 3 * C), C ** -0.5, 0.4375),
        "w_proj": noise(splits[5], (C, C), C ** -0.5, 0.4375),
        "w_up": noise(splits[6], (C, FF), C ** -0.5, 0.4375),
        "w_down": noise(splits[7], (FF, C), FF ** -0.5, 0.21875),
        "gains": jnp.clip(1.0 + 0.18 * jax.random.normal(splits[8], (2, C), jnp.float32), 0.1, 1.9),
        "earth_bias": noise(splits[9], (NLATW, HEADS, BIAS_POS), 1.0, 4.0, ((0, 8),), jnp.float32),
    }


EPS = 1e-05

def windows(block):
    levels, rows, cols, depth = block.shape
    shaped = block.reshape(levels // WIN_PL, WIN_PL, rows // WIN_LAT, WIN_LAT, cols // WIN_LON, WIN_LON, depth)
    shaped = shaped.transpose(0, 2, 4, 1, 3, 5, 6)
    return shaped.reshape(-1, WIN_PL * WIN_LAT * WIN_LON, depth)

def unwindows(tiles, levels, rows, cols):
    depth = tiles.shape[-1]
    shaped = tiles.reshape(levels // WIN_PL, rows // WIN_LAT, cols // WIN_LON, WIN_PL, WIN_LAT, WIN_LON, depth)
    shaped = shaped.transpose(0, 3, 1, 4, 2, 5, 6)
    return shaped.reshape(levels, rows, cols, depth)

def layer_norm(source, gain):
    centre = source - lax.optimization_barrier(jnp.mean(source, axis=-1, keepdims=True))
    recip = lax.rsqrt(lax.optimization_barrier(jnp.mean(centre * centre, axis=-1, keepdims=True)) + EPS)
    normed = centre * recip
    return (normed, recip, normed * gain)

def norm_back(upper, normed, recip, gain):
    lowered = upper * gain
    return recip * (lowered - lax.optimization_barrier(jnp.mean(lowered, axis=-1, keepdims=True)) - normed * lax.optimization_barrier(jnp.mean(lowered * normed, axis=-1, keepdims=True)))

def gelu_parts(upward):
    cumulative = 0.5 * (1.0 + lax.erf(upward * 0.7071067811865476))
    density = jnp.exp(-0.5 * upward * upward) * 0.3989422804014327
    return (upward * cumulative, cumulative + upward * density)

def product(form, left, right):
    return jnp.einsum(form, left.astype(jnp.float32), right.astype(jnp.float32))

def matmul(left, right):
    return jnp.dot(left, right, preferred_element_type=jnp.float32)

def block_grads(states, cotan, labels, table, pos_index, w_qkv, w_proj, w_up, w_down, gains):
    levels, rows, cols, width = states.shape
    head_size = width // HEADS
    scale = head_size ** (-0.5)
    span = WIN_PL * WIN_LAT * WIN_LON
    flat_in = windows(states).reshape(-1, width)
    count = flat_in.shape[0]
    nwin = count // span
    groups = (levels // WIN_PL, rows // WIN_LAT, cols // WIN_LON)
    label_grid = jnp.broadcast_to(labels.T[:, :, None, None], (levels, rows, cols, 1))
    win_labels = windows(label_grid)[..., 0]
    same = win_labels[:, :, None] == win_labels[:, None, :]
    normed_one, recip_one, scaled_one = layer_norm(flat_in.astype(jnp.float32), gains[0])
    hidden_one = scaled_one.astype(jnp.bfloat16)
    triple = matmul(hidden_one, w_qkv).astype(jnp.bfloat16).reshape(nwin, span, 3, HEADS, head_size)
    query = triple[:, :, 0]
    keys = triple[:, :, 1]
    values_h = triple[:, :, 2]
    earth = jnp.take(table, pos_index, axis=2)
    scores = product('wqhd,wkhd->whqk', query, keys) * scale
    scores = (scores.reshape(groups + (HEADS, span, span)) + earth[None, :, None]).reshape(nwin, HEADS, span, span)
    expo = jnp.where(same[:, None], jnp.exp(scores), 0.0)
    probs = expo / lax.optimization_barrier(jnp.sum(expo, axis=-1, keepdims=True))
    probs_low = probs.astype(jnp.bfloat16)
    attended = product('whqk,wkhd->wqhd', probs_low, values_h).astype(jnp.bfloat16).reshape(count, width)
    mixed = flat_in.astype(jnp.float32) + matmul(attended, w_proj)
    resid = mixed.astype(jnp.bfloat16)
    normed_two, recip_two, scaled_two = layer_norm(resid.astype(jnp.float32), gains[1])
    hidden_two = scaled_two.astype(jnp.bfloat16)
    upward = matmul(hidden_two, w_up)
    acted, slope = gelu_parts(upward)
    acted_low = acted.astype(jnp.bfloat16)
    grad_out = windows(cotan).reshape(count, width)
    grad_down = matmul(acted_low.T, grad_out)
    grad_act = (matmul(grad_out, w_down.T) * slope).astype(jnp.bfloat16)
    grad_up = matmul(hidden_two.T, grad_act)
    grad_hid_two = matmul(grad_act, w_up.T)
    gain_two = lax.optimization_barrier(jnp.sum(grad_hid_two * normed_two, axis=0))
    grad_resid = (grad_out.astype(jnp.float32) + norm_back(grad_hid_two, normed_two, recip_two, gains[1])).astype(jnp.bfloat16)
    grad_proj = matmul(attended.T, grad_resid)
    grad_att = matmul(grad_resid, w_proj.T).astype(jnp.bfloat16).reshape(nwin, span, HEADS, head_size)
    grad_prob = product('wqhd,wkhd->whqk', grad_att, values_h)
    grad_score = probs * (grad_prob - lax.optimization_barrier(jnp.sum(probs * grad_prob, axis=-1, keepdims=True)))
    per_type = lax.optimization_barrier(jnp.sum(grad_score.reshape(groups + (HEADS, span, span)), axis=(0, 2)))
    spread = per_type.reshape(groups[1] * HEADS, span * span).T
    grad_table = jax.ops.segment_sum(spread, pos_index.reshape(-1), num_segments=table.shape[2]).T.reshape(groups[1], HEADS, table.shape[2])
    grad_low = (grad_score * scale).astype(jnp.bfloat16)
    grad_val = product('whqk,wqhd->wkhd', probs_low, grad_att).astype(jnp.bfloat16)
    grad_query = product('whqk,wkhd->wqhd', grad_low, keys).astype(jnp.bfloat16)
    grad_keys = product('whqk,wqhd->wkhd', grad_low, query).astype(jnp.bfloat16)
    grad_triple = jnp.stack([grad_query, grad_keys, grad_val], axis=2).reshape(count, 3 * width)
    grad_qkv = matmul(hidden_one.T, grad_triple)
    grad_hid_one = matmul(grad_triple, w_qkv.T)
    gain_one = lax.optimization_barrier(jnp.sum(grad_hid_one * normed_one, axis=0))
    grad_in = (grad_resid.astype(jnp.float32) + norm_back(grad_hid_one, normed_one, recip_one, gains[0])).astype(jnp.bfloat16)
    grad_block = unwindows(grad_in.reshape(nwin, span, width), levels, rows, cols)
    return (grad_block, (grad_qkv, grad_proj, grad_up, grad_down, jnp.stack([gain_one, gain_two])), grad_table)

def reference(states, cotangent, region, pos_index, w_qkv, w_proj, w_up, w_down, gains, earth_bias):
    shifts = (-(WIN_PL // 2), -(WIN_LAT // 2), -(WIN_LON // 2))
    backs = (WIN_PL // 2, WIN_LAT // 2, WIN_LON // 2)
    grid = jnp.roll(states.reshape(MEMBERS, PL, NLAT, NLON, C), shifts, axis=(1, 2, 3))
    cotan = jnp.roll(cotangent.reshape(MEMBERS, PL, NLAT, NLON, C), shifts, axis=(1, 2, 3))
    blocks = NLAT // WIN_LAT

    def step(carry, index):
        member = index // blocks
        start = index % blocks * WIN_LAT
        zero = jnp.zeros((), jnp.int32)
        piece = lax.dynamic_slice(grid, (member, zero, start, zero, zero), (1, PL, WIN_LAT, NLON, C))[0]
        cot_piece = lax.dynamic_slice(cotan, (member, zero, start, zero, zero), (1, PL, WIN_LAT, NLON, C))[0]
        labels = lax.dynamic_slice(region, (start, zero), (WIN_LAT, PL))
        table = lax.dynamic_slice(earth_bias, (index % blocks, zero, zero), (1, HEADS, BIAS_POS))
        grad_block, grads, grad_table = block_grads(piece, cot_piece, labels, table, pos_index, w_qkv, w_proj, w_up, w_down, gains)
        return (jax.tree.map(jnp.add, carry, grads), (grad_block, grad_table))
    init = (jnp.zeros((C, 3 * C), jnp.float32), jnp.zeros((C, C), jnp.float32), jnp.zeros((C, FF), jnp.float32), jnp.zeros((FF, C), jnp.float32), jnp.zeros((2, C), jnp.float32))
    totals, outputs = lax.scan(step, init, jnp.arange(MEMBERS * blocks, dtype=jnp.int32))
    grad_blocks, table_blocks = outputs
    grad_grid = grad_blocks.reshape(MEMBERS, blocks, PL, WIN_LAT, NLON, C).transpose(0, 2, 1, 3, 4, 5)
    grad_grid = jnp.roll(grad_grid.reshape(MEMBERS, PL, NLAT, NLON, C), backs, axis=(1, 2, 3))
    grad_states = grad_grid.reshape(MEMBERS, PL, NLAT, NLON * C)
    grad_bias = table_blocks.reshape(MEMBERS, blocks, HEADS, BIAS_POS).sum(axis=0)
    factor = float(MEMBERS * PL * NLAT * NLON) ** (-0.5)
    return (grad_states, totals[0] * factor, totals[1] * factor, totals[2] * factor, totals[3] * factor, totals[4] * factor, grad_bias)
```

```python
import jax
import jax.numpy as jnp
from jax import lax
from jax.experimental import pallas as pl
from jax.experimental.pallas import tpu as pltpu
from jax.sharding import Mesh
from jax.sharding import PartitionSpec as P

HEADS = 6
SIZE = 32
WIDTH = 192
WIN = 144
CELLS = 288
WIN_PL = 2
WIN_LAT = 6
WIN_LON = 12
BIAS_POS = 3312
CHUNKS = 26
LANES = 128
EPS = 1e-05
X, Y, Z = 4, 4, 16
XY = X * Y
HALF = 1792
PIECE = HALF // XY
BIAS_PIECE = HEADS * 32 // XY
ALL = ("x", "z", "y", "c", "m")
PLANE = ("x", "m", "y")
BF = jnp.bfloat16
F32 = jnp.float32


def nn(left, right):
    return lax.dot_general(left, right, (((1,), (0,)), ((), ())), preferred_element_type=F32)


def nt(left, right):
    return lax.dot_general(left, right, (((1,), (1,)), ((), ())), preferred_element_type=F32)


def tn(left, right):
    return lax.dot_general(left, right, (((0,), (0,)), ((), ())), preferred_element_type=F32)


def layer_norm(source, gain):
    centre = source - jnp.mean(source, axis=-1, keepdims=True)
    recip = lax.rsqrt(jnp.mean(centre * centre, axis=-1, keepdims=True) + EPS)
    normed = centre * recip
    return (normed, recip, normed * gain)


def norm_back(upper, normed, recip, gain):
    lowered = upper * gain
    return recip * (
        lowered
        - jnp.mean(lowered, axis=-1, keepdims=True)
        - normed * jnp.mean(lowered * normed, axis=-1, keepdims=True)
    )


def gelu_parts(upward):
    cumulative = 0.5 * (1.0 + lax.erf(upward * 0.7071067811865476))
    density = jnp.exp(-0.5 * upward * upward) * 0.3989422804014327
    return (upward * cumulative, cumulative + upward * density)


def bias_kernel(pos_ref, table_ref, earth_ref):
    def eight_rows(r, carry):
        rows = pl.ds(pl.multiple_of(r * 8, 8), 8)
        for start, width in ((0, LANES), (LANES, WIN - LANES)):
            place = pos_ref[rows, start : start + LANES]
            low = place & (LANES - 1)
            high = place >> 7
            found = [jnp.zeros((8, LANES), F32) for _ in range(HEADS)]
            for c in range(CHUNKS):
                here = high == c
                for h in range(HEADS):
                    at = h * CHUNKS + c
                    row = jnp.broadcast_to(table_ref[at : at + 1, :], (8, LANES))
                    taken = jnp.take_along_axis(row, low, axis=1, mode="promise_in_bounds")
                    found[h] = jnp.where(here, taken, found[h])
            for h in range(HEADS):
                earth_ref[h, rows, start : start + width] = found[h][:, :width]
        return carry

    lax.fori_loop(0, WIN // 8, eight_rows, 0)


def scatter_kernel(pos_ref, score_ref, table_ref, place_ref, rest_ref):
    which = lax.broadcasted_iota(jnp.int32, (LANES, LANES), 0)
    chunk = lax.broadcasted_iota(jnp.int32, (32, LANES), 0)
    tail = WIN - LANES

    def product(places, scores):
        left, right = [], []
        for n in range(8):
            place = places[n : n + 1]
            right.append(jnp.where(which == (place & (LANES - 1)), 1.0, 0.0).astype(BF))
            here = chunk == (place >> 7)
            parts = [jnp.where(here, score[n : n + 1], 0.0).astype(BF) for score in scores]
            left.append(jnp.concatenate(parts, axis=0))
        return nt(jnp.concatenate(left, axis=1), jnp.concatenate(right, axis=1))

    place_ref[...] = jnp.zeros_like(place_ref)
    rest_ref[...] = jnp.zeros_like(rest_ref)
    place_ref[:, :WIN] = pos_ref[:, LANES:].T
    for h in range(HEADS):
        rest_ref[h, :, :WIN] = score_ref[h, :, LANES:].T
    total = jnp.zeros((HEADS * 32, LANES), F32)
    for k in range(2):
        for at in range(0, tail, 8):
            lanes = slice(k * LANES, (k + 1) * LANES)
            total += product(
                place_ref[at : at + 8, lanes], [rest_ref[h, at : at + 8, lanes] for h in range(HEADS)]
            )
    table_ref[...] = total

    def eight_rows(r, carry):
        rows = pl.ds(pl.multiple_of(r * 8, 8), 8)
        table_ref[...] += product(
            pos_ref[rows, :LANES], [score_ref[h, rows, :LANES] for h in range(HEADS)]
        )
        return carry

    lax.fori_loop(0, WIN // 8, eight_rows, 0, unroll=2)


def block_kernel(
    region_ref, core_ref, x_ref, g_ref, earth_ref, qkv_ref, proj_ref, up_ref, down_ref, gains_ref,
    grad_ref, send_ref, keep_ref, score_ref, triple_ref, wide_ref, gain_ref,
):
    scale = SIZE ** (-0.5)
    x = x_ref[...].astype(F32)
    g_low = g_ref[...]
    gain_a, gain_b = gains_ref[0:1, :], gains_ref[1:2, :]
    normed_one, recip_one, scaled_one = layer_norm(x, gain_a)
    hidden_one = scaled_one.astype(BF)
    triple = nn(hidden_one, qkv_ref[...]).astype(BF)
    head_of = lax.broadcasted_iota(jnp.int32, (1, WIDTH), 1) // SIZE
    masks = [(head_of == h) for h in range(HEADS)]

    def stacked(part):
        return jnp.concatenate([jnp.where(m, part, jnp.zeros_like(part)) for m in masks], axis=0)

    def joined(full):
        full = full.reshape(HEADS, WIN, WIDTH)
        total = jnp.where(masks[0], full[0], 0.0)
        for h in range(1, HEADS):
            total = jnp.where(masks[h], full[h], total)
        return total

    kept = []
    earth = earth_ref[...]
    group_row = lax.broadcasted_iota(jnp.int32, (1, WIN), 1) // WIN_LON
    group_col = lax.broadcasted_iota(jnp.int32, (WIN, 1), 0) // WIN_LON
    attended = []
    for w in range(2):
        rows = slice(w * WIN, (w + 1) * WIN)
        part = triple[rows]
        query, keys, vals = part[:, :WIDTH], part[:, WIDTH : 2 * WIDTH], part[:, 2 * WIDTH :]
        label_row = jnp.zeros((1, WIN), jnp.int32)
        label_col = jnp.zeros((WIN, 1), jnp.int32)
        for group in range(WIN_PL * WIN_LAT):
            label = region_ref[group % WIN_LAT, w * WIN_PL + group // WIN_LAT]
            label_row = jnp.where(group_row == group, label, label_row)
            label_col = jnp.where(group_col == group, label, label_col)
        same = label_row == label_col
        q_stack = stacked(query)
        scores = nt(q_stack, keys).reshape(HEADS, WIN, WIN) * scale + earth
        expo = jnp.where(same[None], jnp.exp(scores), 0.0)
        probs = expo / jnp.sum(expo, axis=-1, keepdims=True)
        probs_low = probs.astype(BF).reshape(HEADS * WIN, WIN)
        attended.append(joined(nn(probs_low, vals)).astype(BF))
        kept.append((q_stack, keys, vals, probs, probs_low))
    attended = jnp.concatenate(attended, axis=0)

    resid = (x + nn(attended, proj_ref[...])).astype(BF)
    normed_two, recip_two, scaled_two = layer_norm(resid.astype(F32), gain_b)
    hidden_two = scaled_two.astype(BF)
    acted, slope = gelu_parts(nn(hidden_two, up_ref[...]))
    acted_low = acted.astype(BF)
    down = tn(g_low, acted_low)
    grad_act = (nn(g_low, down_ref[...]) * slope).astype(BF)
    up = tn(hidden_two, grad_act)
    grad_hid_two = nt(grad_act, up_ref[...])
    gain_ref[...] = jnp.zeros_like(gain_ref)
    gain = jnp.sum(grad_hid_two * normed_two, axis=0, keepdims=True)
    gain_ref[2:3, :] = gain[:, :LANES]
    gain_ref[3:4, : WIDTH - LANES] = gain[:, LANES:]
    grad_resid = (
        g_low.astype(F32) + norm_back(grad_hid_two, normed_two, recip_two, gain_b)
    ).astype(BF)
    wide_ref[:, 3 * WIDTH :] = tn(attended, grad_resid)
    grad_att = nt(grad_resid, proj_ref[...]).astype(BF)
    total = None
    for w in range(2):
        rows = slice(w * WIN, (w + 1) * WIN)
        q_stack, keys, vals, probs, probs_low = kept[w]
        a_stack = stacked(grad_att[rows])
        grad_prob = nt(a_stack, vals).reshape(HEADS, WIN, WIN)
        grad_score = probs * (grad_prob - jnp.sum(probs * grad_prob, axis=-1, keepdims=True))
        total = grad_score if total is None else total + grad_score
        grad_low = (grad_score * scale).astype(BF).reshape(HEADS * WIN, WIN)
        triple_ref[rows, :WIDTH] = joined(nn(grad_low, keys)).astype(BF)
        triple_ref[rows, WIDTH : 2 * WIDTH] = tn(grad_low, q_stack).astype(BF)
        triple_ref[rows, 2 * WIDTH :] = tn(probs_low, a_stack).astype(BF)
    score_ref[...] = total
    grad_triple = triple_ref[...]
    wide_ref[:, : 3 * WIDTH] = tn(hidden_one, grad_triple)
    grad_hid_one = nt(grad_triple, qkv_ref[...])
    gain = jnp.sum(grad_hid_one * normed_one, axis=0, keepdims=True)
    gain_ref[0:1, :] = gain[:, :LANES]
    gain_ref[1:2, : WIDTH - LANES] = gain[:, LANES:]
    grad_ref[...] = (
        grad_resid.astype(F32) + norm_back(grad_hid_one, normed_one, recip_one, gain_a)
    ).astype(BF)
    lines = {}
    for part, whole in enumerate((wide_ref[...], up, down)):
        for k in range(6):
            lines[part * 6 + k] = whole[:, k * LANES : (k + 1) * LANES].astype(BF)
    extra = [jnp.zeros((HALF - 9 * WIDTH, LANES), BF), gain_ref[...].astype(BF)]

    def put(ref, half):
        for k in range(9):
            ref[k * WIDTH : (k + 1) * WIDTH, :] = lines[half * 9 + k]
        ref[9 * WIDTH :, :] = extra[half]

    core = core_ref[0]
    for mine in range(2):

        @pl.when(core == mine)
        def _():
            put(keep_ref, mine)
            put(send_ref, 1 - mine)


def first_sum_kernel(keep_ref, came_ref, table_ref, out_ref, pad_ref):
    pad_ref[...] = jnp.zeros_like(pad_ref)
    for p in range(XY):
        rows = slice(p * PIECE, (p + 1) * PIECE)
        out_ref[p, :PIECE, :] = (keep_ref[rows, :].astype(F32) + came_ref[rows, :].astype(F32)).astype(BF)
        pad_ref[p, :BIAS_PIECE, :] = table_ref[p * BIAS_PIECE : (p + 1) * BIAS_PIECE, :]
        out_ref[p, PIECE:, :] = pad_ref[p].astype(BF)


def second_sum_kernel(came_ref, out_ref, terms_ref, table_ref, pad_ref):
    came = came_ref[...].astype(F32)
    terms_ref[...] = jnp.sum(came[:, :PIECE], axis=0)
    for y in range(Y):
        part = came[y, PIECE:]
        for x in range(1, X):
            part = part + came[x * Y + y, PIECE:]
        table_ref[y * BIAS_PIECE : (y + 1) * BIAS_PIECE, :] = part[:BIAS_PIECE]
    pad_ref[...] = jnp.zeros_like(pad_ref)
    few, less = PIECE // Z, Y * BIAS_PIECE // Z
    for z in range(Z):
        pad_ref[z, :few, :] = terms_ref[z * few : (z + 1) * few, :]
        pad_ref[z, 8 : 8 + less, :] = table_ref[z * less : (z + 1) * less, :]
    out_ref[...] = pad_ref[...].astype(BF)


def third_sum_kernel(came_ref, out_ref):
    total = jnp.sum(came_ref[...].astype(F32), axis=0).astype(BF)
    for z in range(Z):
        out_ref[z] = total


def fan_kernel(came_ref, out_ref, came_wide_ref, terms_ref, table_ref):
    came_wide_ref[...] = came_ref[...].astype(F32)
    table_ref[...] = jnp.zeros_like(table_ref)
    few, less = PIECE // Z, Y * BIAS_PIECE // Z
    for z in range(Z):
        terms_ref[z * few : (z + 1) * few, :] = came_wide_ref[z, :few, :]
        y, at = z * less // BIAS_PIECE, z * less % BIAS_PIECE
        table_ref[y, at : at + less, :] = came_wide_ref[z, 8 : 8 + less, :]
    terms = terms_ref[...].astype(BF)
    for p in range(XY):
        out_ref[p, :PIECE, :] = terms
        out_ref[p, PIECE:, :] = table_ref[p % Y].astype(BF)


def finish_kernel(
    factor, both_ref, mine_ref, qkv_ref, proj_ref, up_ref, down_ref, gains_ref, bias_ref, flat_ref, wide_ref,
):
    for half in range(2):
        for p in range(XY):
            flat_ref[half, p * PIECE : (p + 1) * PIECE, :] = both_ref[half, p, :PIECE, :]

    def block(k):
        rows = slice(k % 9 * WIDTH, (k % 9 + 1) * WIDTH)
        return flat_ref[k // 9, rows, :].astype(F32) * factor

    for k in range(6):
        lanes = slice(k * LANES, (k + 1) * LANES)
        wide_ref[:, lanes] = block(k)
        up_ref[:, lanes] = block(6 + k)
        down_ref[:, lanes] = block(12 + k)
    qkv_ref[...] = wide_ref[:, : 3 * WIDTH]
    proj_ref[...] = wide_ref[:, 3 * WIDTH :]
    gains = flat_ref[1, 9 * WIDTH :, :].astype(F32) * factor
    for n in range(2):
        gains_ref[n : n + 1, :LANES] = gains[2 * n : 2 * n + 1]
        gains_ref[n : n + 1, LANES:] = gains[2 * n + 1 : 2 * n + 2, : WIDTH - LANES]
    for p in range(XY):
        piece = mine_ref[p, PIECE:, :].astype(F32)
        for r in range(BIAS_PIECE):
            h, c = divmod(p * BIAS_PIECE + r, 32)
            width = min(LANES, BIAS_POS - c * LANES)
            if width > 0:
                bias_ref[h : h + 1, c * LANES : c * LANES + width] = piece[r : r + 1, :width]


VMEM = pl.BlockSpec(memory_space=pltpu.VMEM)
SMEM = pl.BlockSpec(memory_space=pltpu.SMEM)


def kernel(function, name, outs, scratch=(), scalars=0, flops=1_000_000, moved=1_000_000):
    shapes = tuple(jax.ShapeDtypeStruct(s, t) for s, t in outs)

    def call(*args):
        return pl.pallas_call(
            function,
            out_shape=shapes,
            in_specs=[SMEM] * scalars + [VMEM] * (len(args) - scalars),
            out_specs=(VMEM,) * len(shapes),
            scratch_shapes=[pltpu.VMEM(s, t) for s, t in scratch],
            compiler_params=pltpu.CompilerParams(vmem_limit_bytes=48 * 1024 * 1024),
            cost_estimate=pl.CostEstimate(flops=flops, bytes_accessed=moved, transcendentals=0),
            name=name,
        )(*args)

    return call


find_bias = kernel(bias_kernel, "find_bias", [((HEADS, WIN, WIN), F32)], flops=20_000_000)
spread_bias = kernel(
    scatter_kernel,
    "spread_bias",
    [((HEADS * 32, LANES), F32)],
    [((WIN - LANES, 2 * LANES), jnp.int32), ((HEADS, WIN - LANES, 2 * LANES), F32)],
    flops=1_000_000_000,
)
block_grads = kernel(
    block_kernel,
    "block_grads",
    [((CELLS, WIDTH), BF), ((HALF, LANES), BF), ((HALF, LANES), BF), ((HEADS, WIN, WIN), F32)],
    [((CELLS, 3 * WIDTH), BF), ((WIDTH, 4 * WIDTH), F32), ((HALF - 9 * WIDTH, LANES), F32)],
    scalars=2,
    flops=1_000_000_000,
    moved=4_000_000,
)
first_sum = kernel(first_sum_kernel, "first_sum", [((XY, LANES, LANES), BF)], [((XY, 16, LANES), F32)])
second_sum = kernel(
    second_sum_kernel,
    "second_sum",
    [((Z, 16, LANES), BF)],
    [((PIECE, LANES), F32), ((Y * BIAS_PIECE, LANES), F32), ((Z, 16, LANES), F32)],
)
third_sum = kernel(third_sum_kernel, "third_sum", [((Z, 16, LANES), BF)])
fan = kernel(
    fan_kernel,
    "fan",
    [((XY, LANES, LANES), BF)],
    [((Z, 16, LANES), F32), ((PIECE, LANES), F32), ((Y, 16, LANES), F32)],
)


def finish(factor, both, mine):
    return kernel(
        lambda *refs: finish_kernel(factor, *refs),
        "finish",
        [
            ((WIDTH, 3 * WIDTH), F32),
            ((WIDTH, WIDTH), F32),
            ((WIDTH, 4 * WIDTH), F32),
            ((WIDTH, 4 * WIDTH), F32),
            ((2, WIDTH), F32),
            ((HEADS, BIAS_POS), F32),
        ],
        [((2, HALF, LANES), BF), ((WIDTH, 4 * WIDTH), F32)],
    )(both, mine)


def routes(lon_step, lat_step):
    lon, lat, mem = 2 * Z, 2 * Y, 2
    return [
        ((a * lat + b) * mem + c, ((a + lon_step) % lon * lat + (b + lat_step) % lat) * mem + c)
        for a in range(lon)
        for b in range(lat)
        for c in range(mem)
    ]


def shifted(pair):
    half_rows, half_cols = pair.shape[2] // 2, pair.shape[3] // 2
    pair = jnp.roll(pair, -1, axis=1)
    own, east = pair[:, :, half_rows:, half_cols:], pair[:, :, half_rows:, :half_cols]
    south, corner = pair[:, :, :half_rows, half_cols:], pair[:, :, :half_rows, :half_cols]
    corner = lax.ppermute(corner, ALL, routes(-1, -1))
    east = lax.ppermute(east, ALL, routes(-1, 0))
    south = lax.ppermute(south, ALL, routes(0, -1))
    top = jnp.concatenate([own, east], axis=3)
    bottom = jnp.concatenate([south, corner], axis=3)
    return jnp.concatenate([top, bottom], axis=2)


def unshifted(grad):
    half_rows, half_cols = grad.shape[1] // 2, grad.shape[2] // 2
    grad = jnp.roll(grad, 1, axis=0)
    own, east = grad[:, :half_rows, :half_cols], grad[:, :half_rows, half_cols:]
    south, corner = grad[:, half_rows:, :half_cols], grad[:, half_rows:, half_cols:]
    corner = lax.ppermute(corner, ALL, routes(1, 1))
    east = lax.ppermute(east, ALL, routes(1, 0))
    south = lax.ppermute(south, ALL, routes(0, 1))
    top = jnp.concatenate([corner, south], axis=2)
    bottom = jnp.concatenate([east, own], axis=2)
    return jnp.concatenate([top, bottom], axis=1)


def body(states, cotangent, region, pos_index, w_qkv, w_proj, w_up, w_down, gains, earth_bias):
    levels, rows, merged = states.shape[1:]
    place = jnp.pad(pos_index, ((0, 0), (0, 2 * LANES - WIN)))
    table = jnp.pad(earth_bias[0], ((0, 0), (0, CHUNKS * LANES - BIAS_POS)))
    (earth,) = find_bias(place, table.reshape(HEADS * CHUNKS, LANES))
    pair = shifted(jnp.concatenate([states, cotangent], axis=0))
    cells = pair.reshape(2, CELLS, WIDTH)
    core = lax.axis_index("c").astype(jnp.int32).reshape(1)
    grad, send, keep, score = block_grads(
        region, core, cells[0], cells[1], earth, w_qkv, w_proj, w_up, w_down.T, gains
    )
    came = lax.ppermute(send, "c", [(0, 1), (1, 0)])
    grad_states = unshifted(grad.reshape(levels, rows, merged))[None]
    (spread,) = spread_bias(pos_index, score)
    (plane,) = first_sum(keep, came, spread)
    plane = lax.all_to_all(plane, PLANE, 0, 0)
    (line,) = second_sum(plane)
    line = lax.all_to_all(line, "z", 0, 0)
    (line,) = third_sum(line)
    line = lax.all_to_all(line, "z", 0, 0)
    (plane,) = fan(line)
    plane = lax.all_to_all(plane, PLANE, 0, 0)
    both = lax.all_gather(plane, "c")
    factor = float(CELLS * lax.axis_size(ALL)) ** (-0.5)
    grad_qkv, grad_proj, grad_up, grad_down, grad_gains, grad_bias = finish(factor, both, plane)
    return (grad_states, grad_qkv, grad_proj, grad_up, grad_down.T, grad_gains, grad_bias[None])


def solution(mesh):
    fine = Mesh(mesh.devices.reshape(2, Z, Y, 2, 2), ALL)
    lon, lat = ("x", "z"), ("y", "c")
    return jax.shard_map(
        body,
        mesh=fine,
        in_specs=(
            P("m", None, lat, lon),
            P("m", None, lat, lon),
            P(lat, None),
            P(),
            P(),
            P(),
            P(),
            P(),
            P(),
            P(lat, None, None),
        ),
        out_specs=(P("m", None, lat, lon), P(), P(), P(), P(), P(), P(lat, None, None)),
        check_vma=False,
    )
```

```python
import jax
import jax.numpy as jnp
from jax import lax
from jax.experimental import pallas as pl
from jax.experimental.pallas import tpu as pltpu
from jax.sharding import Mesh
from jax.sharding import PartitionSpec as P

HEADS = 6
SIZE = 32
WIDTH = 192
WIN = 144
CELLS = 288
WIN_PL = 2
WIN_LAT = 6
WIN_LON = 12
BIAS_POS = 3312
CHUNKS = 26
LANES = 128
EPS = 1e-05
Y, Z, FAR = 4, 16, 8
NEAR = 32
HALF = 1792
PIECE = HALF // NEAR
BIAS_PIECE = HEADS * 32 // NEAR
LINE = PIECE + Y * BIAS_PIECE
ALL = ("x", "far", "pair", "y", "c", "m")
PLANE = ("x", "m", "y", "pair")
SWAP = [(0, 1), (1, 0)]
BF = jnp.bfloat16
F32 = jnp.float32


def nn(left, right):
    return lax.dot_general(left, right, (((1,), (0,)), ((), ())), preferred_element_type=F32)


def nt(left, right):
    return lax.dot_general(left, right, (((1,), (1,)), ((), ())), preferred_element_type=F32)


def tn(left, right):
    return lax.dot_general(left, right, (((0,), (0,)), ((), ())), preferred_element_type=F32)


def layer_norm(source, gain):
    centre = source - jnp.mean(source, axis=-1, keepdims=True)
    recip = lax.rsqrt(jnp.mean(centre * centre, axis=-1, keepdims=True) + EPS)
    normed = centre * recip
    return (normed, recip, normed * gain)


def norm_back(upper, normed, recip, gain):
    lowered = upper * gain
    return recip * (
        lowered
        - jnp.mean(lowered, axis=-1, keepdims=True)
        - normed * jnp.mean(lowered * normed, axis=-1, keepdims=True)
    )


def gelu_parts(upward):
    cumulative = 0.5 * (1.0 + lax.erf(upward * 0.7071067811865476))
    density = jnp.exp(-0.5 * upward * upward) * 0.3989422804014327
    return (upward * cumulative, cumulative + upward * density)


def bias_kernel(pos_ref, table_ref, earth_ref, place_ref, rest_ref):
    tail = WIN - LANES

    def looked_up(place):
        low = place & (LANES - 1)
        high = place >> 7
        found = [jnp.zeros((8, LANES), F32) for _ in range(HEADS)]
        for c in range(CHUNKS):
            here = high == c
            for h in range(HEADS):
                row = table_ref[h : h + 1, c * LANES : min((c + 1) * LANES, BIAS_POS)]
                if row.shape[1] < LANES:
                    row = jnp.concatenate([row, jnp.zeros((1, LANES - row.shape[1]), F32)], axis=1)
                row = jnp.broadcast_to(row, (8, LANES))
                taken = jnp.take_along_axis(row, low, axis=1, mode="promise_in_bounds")
                found[h] = jnp.where(here, taken, found[h])
        return found

    def eight_rows(r, carry):
        rows = pl.ds(pl.multiple_of(r * 8, 8), 8)
        found = looked_up(pos_ref[rows, :LANES])
        for h in range(HEADS):
            earth_ref[h, rows, :LANES] = found[h]
        return carry

    lax.fori_loop(0, WIN // 8, eight_rows, 0)
    place_ref[...] = jnp.zeros_like(place_ref)
    place_ref[:, :WIN] = pos_ref[:, LANES:].T

    def eight_columns(r, carry):
        rows = pl.ds(pl.multiple_of(r * 8, 8), 8)
        for k in range(2):
            lanes = slice(k * LANES, (k + 1) * LANES)
            found = looked_up(place_ref[rows, lanes])
            for h in range(HEADS):
                rest_ref[h, rows, lanes] = found[h]
        return carry

    lax.fori_loop(0, tail // 8, eight_columns, 0)
    for h in range(HEADS):
        earth_ref[h, :, LANES:] = rest_ref[h, :, :WIN].T


def scatter_kernel(pos_ref, score_ref, table_ref, place_ref, rest_ref):
    which = lax.broadcasted_iota(jnp.int32, (LANES, LANES), 0)
    chunk = lax.broadcasted_iota(jnp.int32, (32, LANES), 0)
    tail = WIN - LANES

    def product(places, scores):
        left, right = [], []
        for n in range(8):
            place = places[n : n + 1]
            right.append(jnp.where(which == (place & (LANES - 1)), 1.0, 0.0).astype(BF))
            here = chunk == (place >> 7)
            parts = [jnp.where(here, score[n : n + 1], 0.0).astype(BF) for score in scores]
            left.append(jnp.concatenate(parts, axis=0))
        return nt(jnp.concatenate(left, axis=1), jnp.concatenate(right, axis=1))

    place_ref[...] = jnp.zeros_like(place_ref)
    rest_ref[...] = jnp.zeros_like(rest_ref)
    place_ref[:, :WIN] = pos_ref[:, LANES:].T
    for h in range(HEADS):
        rest_ref[h, :, :WIN] = score_ref[h, :, LANES:].T
    total = jnp.zeros((HEADS * 32, LANES), F32)
    for k in range(2):
        for at in range(0, tail, 8):
            lanes = slice(k * LANES, (k + 1) * LANES)
            total += product(
                place_ref[at : at + 8, lanes], [rest_ref[h, at : at + 8, lanes] for h in range(HEADS)]
            )
    table_ref[...] = total

    def eight_rows(r, carry):
        rows = pl.ds(pl.multiple_of(r * 8, 8), 8)
        table_ref[...] += product(
            pos_ref[rows, :LANES], [score_ref[h, rows, :LANES] for h in range(HEADS)]
        )
        return carry

    lax.fori_loop(0, WIN // 8, eight_rows, 0, unroll=2)


def block_kernel(
    region_ref, core_ref, x_ref, g_ref, earth_ref, qkv_ref, proj_ref, up_ref, down_ref, gains_ref,
    grad_ref, send_ref, keep_ref, score_ref, triple_ref, wide_ref, gain_ref,
):
    scale = SIZE ** (-0.5)
    x = x_ref[...].astype(F32)
    g_low = g_ref[...]
    gain_a, gain_b = gains_ref[0:1, :], gains_ref[1:2, :]
    normed_one, recip_one, scaled_one = layer_norm(x, gain_a)
    hidden_one = scaled_one.astype(BF)
    triple = nn(hidden_one, qkv_ref[...]).astype(BF)
    head_of = lax.broadcasted_iota(jnp.int32, (1, WIDTH), 1) // SIZE
    masks = [(head_of == h) for h in range(HEADS)]

    def stacked(part):
        return jnp.concatenate([jnp.where(m, part, jnp.zeros_like(part)) for m in masks], axis=0)

    def joined(full):
        full = full.reshape(HEADS, WIN, WIDTH)
        total = jnp.where(masks[0], full[0], 0.0)
        for h in range(1, HEADS):
            total = jnp.where(masks[h], full[h], total)
        return total

    kept = []
    earth = earth_ref[...]
    group_row = lax.broadcasted_iota(jnp.int32, (1, WIN), 1) // WIN_LON
    group_col = lax.broadcasted_iota(jnp.int32, (WIN, 1), 0) // WIN_LON
    attended = []
    for w in range(2):
        rows = slice(w * WIN, (w + 1) * WIN)
        part = triple[rows]
        query, keys, vals = part[:, :WIDTH], part[:, WIDTH : 2 * WIDTH], part[:, 2 * WIDTH :]
        label_row = jnp.zeros((1, WIN), jnp.int32)
        label_col = jnp.zeros((WIN, 1), jnp.int32)
        for group in range(WIN_PL * WIN_LAT):
            label = region_ref[group % WIN_LAT, w * WIN_PL + group // WIN_LAT]
            label_row = jnp.where(group_row == group, label, label_row)
            label_col = jnp.where(group_col == group, label, label_col)
        same = label_row == label_col
        q_stack = stacked(query)
        scores = nt(q_stack, keys).reshape(HEADS, WIN, WIN) * scale + earth
        expo = jnp.where(same[None], jnp.exp(scores), 0.0)
        probs = expo / jnp.sum(expo, axis=-1, keepdims=True)
        probs_low = probs.astype(BF).reshape(HEADS * WIN, WIN)
        attended.append(joined(nn(probs_low, vals)).astype(BF))
        kept.append((q_stack, keys, vals, probs, probs_low))
    attended = jnp.concatenate(attended, axis=0)

    resid = (x + nn(attended, proj_ref[...])).astype(BF)
    normed_two, recip_two, scaled_two = layer_norm(resid.astype(F32), gain_b)
    hidden_two = scaled_two.astype(BF)
    acted, slope = gelu_parts(nn(hidden_two, up_ref[...]))
    acted_low = acted.astype(BF)
    down = tn(g_low, acted_low)
    grad_act = (nn(g_low, down_ref[...]) * slope).astype(BF)
    up = tn(hidden_two, grad_act)
    grad_hid_two = nt(grad_act, up_ref[...])
    gain_ref[...] = jnp.zeros_like(gain_ref)
    gain = jnp.sum(grad_hid_two * normed_two, axis=0, keepdims=True)
    gain_ref[2:3, :] = gain[:, :LANES]
    gain_ref[3:4, : WIDTH - LANES] = gain[:, LANES:]
    grad_resid = (
        g_low.astype(F32) + norm_back(grad_hid_two, normed_two, recip_two, gain_b)
    ).astype(BF)
    wide_ref[:, 3 * WIDTH :] = tn(attended, grad_resid)
    grad_att = nt(grad_resid, proj_ref[...]).astype(BF)
    total = None
    for w in range(2):
        rows = slice(w * WIN, (w + 1) * WIN)
        q_stack, keys, vals, probs, probs_low = kept[w]
        a_stack = stacked(grad_att[rows])
        grad_prob = nt(a_stack, vals).reshape(HEADS, WIN, WIN)
        grad_score = probs * (grad_prob - jnp.sum(probs * grad_prob, axis=-1, keepdims=True))
        total = grad_score if total is None else total + grad_score
        grad_low = (grad_score * scale).astype(BF).reshape(HEADS * WIN, WIN)
        triple_ref[rows, :WIDTH] = joined(nn(grad_low, keys)).astype(BF)
        triple_ref[rows, WIDTH : 2 * WIDTH] = tn(grad_low, q_stack).astype(BF)
        triple_ref[rows, 2 * WIDTH :] = tn(probs_low, a_stack).astype(BF)
    score_ref[...] = total
    grad_triple = triple_ref[...]
    wide_ref[:, : 3 * WIDTH] = tn(hidden_one, grad_triple)
    grad_hid_one = nt(grad_triple, qkv_ref[...])
    gain = jnp.sum(grad_hid_one * normed_one, axis=0, keepdims=True)
    gain_ref[0:1, :] = gain[:, :LANES]
    gain_ref[1:2, : WIDTH - LANES] = gain[:, LANES:]
    grad_ref[...] = (
        grad_resid.astype(F32) + norm_back(grad_hid_one, normed_one, recip_one, gain_a)
    ).astype(BF)
    lines = {}
    for part, whole in enumerate((wide_ref[...], up, down)):
        for k in range(6):
            lines[part * 6 + k] = whole[:, k * LANES : (k + 1) * LANES].astype(BF)
    extra = [jnp.zeros((HALF - 9 * WIDTH, LANES), BF), gain_ref[...].astype(BF)]

    def put(ref, half):
        for k in range(9):
            ref[k * WIDTH : (k + 1) * WIDTH, :] = lines[half * 9 + k]
        ref[9 * WIDTH :, :] = extra[half]

    core = core_ref[0]
    for mine in range(2):

        @pl.when(core == mine)
        def _():
            put(keep_ref, mine)
            put(send_ref, 1 - mine)


def first_sum_kernel(keep_ref, came_ref, table_ref, out_ref, total_ref, pad_ref):
    total_ref[...] = keep_ref[...].astype(F32) + came_ref[...].astype(F32)
    pad_ref[...] = jnp.zeros_like(pad_ref)
    for p in range(NEAR):
        pad_ref[p, :PIECE, :] = total_ref[p * PIECE : (p + 1) * PIECE, :]
        pad_ref[p, PIECE : PIECE + BIAS_PIECE, :] = table_ref[p * BIAS_PIECE : (p + 1) * BIAS_PIECE, :]
    out_ref[...] = pad_ref[...].astype(BF)


def second_sum_kernel(came_ref, *refs):
    out_ref, line_ref = refs[-2:]
    came = came_ref[...].astype(F32)
    line_ref[:PIECE, :] = jnp.sum(came[:, :PIECE], axis=0)
    table = came[:, PIECE:].reshape(NEAR // Y // 2, Y, 2, 8, LANES)
    table = jnp.sum(jnp.sum(table, axis=2), axis=0)
    for y in range(Y):
        at = PIECE + y * BIAS_PIECE
        line_ref[at : at + BIAS_PIECE, :] = table[y, :BIAS_PIECE]
    line = line_ref[...].astype(BF)
    for n in range(FAR):
        out_ref[n] = line


def fan_kernel(came_ref, out_ref, line_ref, pad_ref):
    line_ref[...] = jnp.sum(came_ref[...].astype(F32), axis=0)
    pad_ref[...] = jnp.zeros_like(pad_ref)
    for y in range(Y):
        at = PIECE + y * BIAS_PIECE
        pad_ref[y, :PIECE, :] = line_ref[:PIECE, :]
        pad_ref[y, PIECE : PIECE + BIAS_PIECE, :] = line_ref[at : at + BIAS_PIECE, :]
    pieces = pad_ref[...].astype(BF)
    for p in range(NEAR):
        out_ref[p] = pieces[p // 2 % Y]


def finish_kernel(
    factor, core_ref, mine_ref, came_ref, qkv_ref, proj_ref, up_ref, down_ref, gains_ref, bias_ref, flat_ref, wide_ref,
):
    core = core_ref[0]
    mine, came = mine_ref[...].astype(F32), came_ref[...].astype(F32)
    for p in range(NEAR):
        rows = slice(p * PIECE, (p + 1) * PIECE)
        flat_ref[core, rows, :] = mine[p, :PIECE] * factor
        flat_ref[1 - core, rows, :] = came[p, :PIECE] * factor

    def block(k):
        rows = slice(k % 9 * WIDTH, (k % 9 + 1) * WIDTH)
        return flat_ref[k // 9, rows, :]

    for k in range(6):
        lanes = slice(k * LANES, (k + 1) * LANES)
        wide_ref[:, lanes] = block(k)
        up_ref[:, lanes] = block(6 + k)
        down_ref[:, lanes] = block(12 + k)
    qkv_ref[...] = wide_ref[:, : 3 * WIDTH]
    proj_ref[...] = wide_ref[:, 3 * WIDTH :]
    gains = flat_ref[1, 9 * WIDTH :, :]
    for n in range(2):
        gains_ref[n : n + 1, :LANES] = gains[2 * n : 2 * n + 1]
        gains_ref[n : n + 1, LANES:] = gains[2 * n + 1 : 2 * n + 2, : WIDTH - LANES]
    for p in range(NEAR):
        piece = mine[p, PIECE:]
        for r in range(BIAS_PIECE):
            h, c = divmod(p * BIAS_PIECE + r, 32)
            width = min(LANES, BIAS_POS - c * LANES)
            if width > 0:
                bias_ref[h : h + 1, c * LANES : c * LANES + width] = piece[r : r + 1, :width]


VMEM = pl.BlockSpec(memory_space=pltpu.VMEM)
SMEM = pl.BlockSpec(memory_space=pltpu.SMEM)
ANY = pl.BlockSpec(memory_space=pl.ANY)


def kernel(function, name, outs, scratch=(), scalars=0, later=0, flops=1_000_000, moved=1_000_000):
    shapes = tuple(jax.ShapeDtypeStruct(s, t) for s, t in outs)

    def call(*args):
        return pl.pallas_call(
            function,
            out_shape=shapes,
            in_specs=[SMEM] * scalars + [VMEM] * (len(args) - scalars - later) + [ANY] * later,
            out_specs=(VMEM,) * len(shapes),
            scratch_shapes=[pltpu.VMEM(s, t) for s, t in scratch],
            compiler_params=pltpu.CompilerParams(vmem_limit_bytes=48 * 1024 * 1024),
            cost_estimate=pl.CostEstimate(flops=flops, bytes_accessed=moved, transcendentals=0),
            name=name,
        )(*args)

    return call


REST = [((WIN - LANES, 2 * LANES), jnp.int32), ((HEADS, WIN - LANES, 2 * LANES), F32)]
find_bias = kernel(bias_kernel, "find_bias", [((HEADS, WIN, WIN), F32)], REST, flops=20_000_000)
spread_bias = kernel(
    scatter_kernel,
    "spread_bias",
    [((HEADS * 32, LANES), F32)],
    REST,
    flops=1_000_000_000,
)
block_grads = kernel(
    block_kernel,
    "block_grads",
    [((CELLS, WIDTH), BF), ((HALF, LANES), BF), ((HALF, LANES), BF), ((HEADS, WIN, WIN), F32)],
    [((CELLS, 3 * WIDTH), BF), ((WIDTH, 4 * WIDTH), F32), ((HALF - 9 * WIDTH, LANES), F32)],
    scalars=2,
    flops=1_000_000_000,
    moved=4_000_000,
)
first_sum = kernel(
    first_sum_kernel, "first_sum", [((NEAR, 64, LANES), BF)], [((HALF, LANES), F32), ((NEAR, 64, LANES), F32)]
)
second_sum = kernel(
    second_sum_kernel, "second_sum", [((FAR, LINE, LANES), BF)], [((LINE, LANES), F32)], later=3
)
fan = kernel(
    fan_kernel, "fan", [((NEAR, 64, LANES), BF)], [((LINE, LANES), F32), ((Y, 64, LANES), F32)]
)


def finish(factor, core, mine, came):
    return kernel(
        lambda *refs: finish_kernel(factor, *refs),
        "finish",
        [
            ((WIDTH, 3 * WIDTH), F32),
            ((WIDTH, WIDTH), F32),
            ((WIDTH, 4 * WIDTH), F32),
            ((WIDTH, 4 * WIDTH), F32),
            ((2, WIDTH), F32),
            ((HEADS, BIAS_POS), F32),
        ],
        [((2, HALF, LANES), F32), ((WIDTH, 4 * WIDTH), F32)],
        scalars=1,
    )(core, mine, came)


def routes(lon_step, lat_step):
    lon, lat, mem = 2 * Z, 2 * Y, 2
    return [
        ((a * lat + b) * mem + c, ((a + lon_step) % lon * lat + (b + lat_step) % lat) * mem + c)
        for a in range(lon)
        for b in range(lat)
        for c in range(mem)
    ]


def shifted(pair):
    half_rows, half_cols = pair.shape[2] // 2, pair.shape[3] // 2
    pair = jnp.roll(pair, -1, axis=1)
    own, east = pair[:, :, half_rows:, half_cols:], pair[:, :, half_rows:, :half_cols]
    south, corner = pair[:, :, :half_rows, half_cols:], pair[:, :, :half_rows, :half_cols]
    corner = lax.ppermute(corner, ALL, routes(-1, -1))
    east = lax.ppermute(east, ALL, routes(-1, 0))
    south = lax.ppermute(south, ALL, routes(0, -1))
    top = jnp.concatenate([own, east], axis=3)
    bottom = jnp.concatenate([south, corner], axis=3)
    return jnp.concatenate([top, bottom], axis=2)


def sent_back(grad):
    half_rows, half_cols = grad.shape[1] // 2, grad.shape[2] // 2
    east, south = grad[:, :half_rows, half_cols:], grad[:, half_rows:, :half_cols]
    corner = grad[:, half_rows:, half_cols:]
    corner = lax.ppermute(corner, ALL, routes(1, 1))
    east = lax.ppermute(east, ALL, routes(1, 0))
    south = lax.ppermute(south, ALL, routes(0, 1))
    return corner, east, south


def unshifted(grad, corner, east, south):
    own = grad[:, : grad.shape[1] // 2, : grad.shape[2] // 2]
    top = jnp.concatenate([corner, south], axis=2)
    bottom = jnp.concatenate([east, own], axis=2)
    return jnp.roll(jnp.concatenate([top, bottom], axis=1), 1, axis=0)


def body(states, cotangent, region, pos_index, w_qkv, w_proj, w_up, w_down, gains, earth_bias):
    levels, rows, merged = states.shape[1:]
    (earth,) = find_bias(pos_index, earth_bias[0])
    pair = shifted(jnp.concatenate([states, cotangent], axis=0))
    cells = pair.reshape(2, CELLS, WIDTH)
    core = lax.axis_index("c").astype(jnp.int32).reshape(1)
    grad, send, keep, score = block_grads(
        region, core, cells[0], cells[1], earth, w_qkv, w_proj, w_up, w_down.T, gains
    )
    came = lax.ppermute(send, "c", SWAP)
    grad = grad.reshape(levels, rows, merged)
    back = sent_back(grad)
    (spread,) = spread_bias(pos_index, score)
    (plane,) = first_sum(keep, came, spread)
    plane = lax.all_to_all(plane, PLANE, 0, 0)
    (line,) = second_sum(plane, *back)
    line = lax.all_to_all(line, "far", 0, 0)
    (plane,) = fan(line)
    plane = lax.all_to_all(plane, PLANE, 0, 0)
    came = lax.ppermute(plane, "c", SWAP)
    factor = float(CELLS * lax.axis_size(ALL)) ** (-0.5)
    grad_qkv, grad_proj, grad_up, grad_down, grad_gains, grad_bias = finish(factor, core, plane, came)
    grad_states = unshifted(grad, *back)[None]
    return (grad_states, grad_qkv, grad_proj, grad_up, grad_down.T, grad_gains, grad_bias[None])


def solution(mesh):
    fine = Mesh(mesh.devices.reshape(2, FAR, 2, Y, 2, 2), ALL)
    lon, lat = ("x", "far", "pair"), ("y", "c")
    return jax.shard_map(
        body,
        mesh=fine,
        in_specs=(
            P("m", None, lat, lon),
            P("m", None, lat, lon),
            P(lat, None),
            P(),
            P(),
            P(),
            P(),
            P(),
            P(),
            P(lat, None, None),
        ),
        out_specs=(P("m", None, lat, lon), P(), P(), P(), P(), P(), P(lat, None, None)),
        check_vma=False,
    )
```

```python
import jax
import jax.numpy as jnp
from jax import lax
from jax.experimental import pallas as pl
from jax.experimental.pallas import tpu as pltpu
from jax.sharding import Mesh
from jax.sharding import PartitionSpec as P

HEADS = 6
SIZE = 32
WIDTH = 192
WIN = 144
CELLS = 288
WIN_PL = 2
WIN_LAT = 6
WIN_LON = 12
BIAS_POS = 3312
CHUNKS = 26
LANES = 128
EPS = 1e-05
Y, Z, FAR = 4, 16, 8
NEAR = 32
HALF = 1792
PIECE = HALF // NEAR
BIAS_PIECE = HEADS * 32 // NEAR
LINE = PIECE + Y * BIAS_PIECE
ALL = ("x", "far", "pair", "y", "c", "m")
PLANE = ("x", "m", "y", "pair")
SWAP = [(0, 1), (1, 0)]
BF = jnp.bfloat16
F32 = jnp.float32


def nn(left, right):
    return lax.dot_general(left, right, (((1,), (0,)), ((), ())), preferred_element_type=F32)


def nt(left, right):
    return lax.dot_general(left, right, (((1,), (1,)), ((), ())), preferred_element_type=F32)


def tn(left, right):
    return lax.dot_general(left, right, (((0,), (0,)), ((), ())), preferred_element_type=F32)


def layer_norm(source, gain):
    centre = source - jnp.mean(source, axis=-1, keepdims=True)
    recip = lax.rsqrt(jnp.mean(centre * centre, axis=-1, keepdims=True) + EPS)
    normed = centre * recip
    return (normed, recip, normed * gain)


def norm_back(upper, normed, recip, gain):
    lowered = upper * gain
    return recip * (
        lowered
        - jnp.mean(lowered, axis=-1, keepdims=True)
        - normed * jnp.mean(lowered * normed, axis=-1, keepdims=True)
    )


def gelu_parts(upward):
    cumulative = 0.5 * (1.0 + lax.erf(upward * 0.7071067811865476))
    density = jnp.exp(-0.5 * upward * upward) * 0.3989422804014327
    return (upward * cumulative, cumulative + upward * density)


def bias_kernel(pos_ref, table_ref, *refs):
    earth_ref, place_ref, rest_ref, pair_ref = refs[-4:]
    tail = WIN - LANES
    pair_ref[...] = jnp.zeros_like(pair_ref)
    for n in range(HEADS // 2):
        first, second = [
            jnp.floor(table_ref[h] * 8191.0 + 0.5).astype(jnp.int32) for h in (2 * n, 2 * n + 1)
        ]
        pair_ref[n : n + 1, :BIAS_POS] = (first << 16) + (second & 65535)

    def looked_up(place):
        low = place & (LANES - 1)
        high = place >> 7
        found = [jnp.zeros((8, LANES), jnp.int32) for _ in range(HEADS // 2)]
        for c in range(CHUNKS):
            here = high == c
            for n in range(HEADS // 2):
                row = jnp.broadcast_to(pair_ref[n : n + 1, c * LANES : (c + 1) * LANES], (8, LANES))
                taken = jnp.take_along_axis(row, low, axis=1, mode="promise_in_bounds")
                found[n] = jnp.where(here, taken, found[n])
        parts = []
        for both in found:
            parts += [both >> 16, (both << 16) >> 16]
        return [part.astype(F32) * (1.0 / 8191.0) for part in parts]

    def eight_rows(r, carry):
        rows = pl.ds(pl.multiple_of(r * 8, 8), 8)
        found = looked_up(pos_ref[rows, :LANES])
        for h in range(HEADS):
            earth_ref[h, rows, :LANES] = found[h]
        return carry

    lax.fori_loop(0, WIN // 8, eight_rows, 0, unroll=2)
    place_ref[...] = jnp.zeros_like(place_ref)
    place_ref[:, :WIN] = pos_ref[:, LANES:].T
    for at in range(0, tail, 8):
        for k in range(2):
            lanes = slice(k * LANES, (k + 1) * LANES)
            found = looked_up(place_ref[at : at + 8, lanes])
            for h in range(HEADS):
                rest_ref[h, at : at + 8, lanes] = found[h]
    for h in range(HEADS):
        earth_ref[h, :, LANES:] = rest_ref[h, :, :WIN].T


def scatter_kernel(pos_ref, score_ref, table_ref, place_ref, rest_ref):
    which = lax.broadcasted_iota(jnp.int32, (LANES, LANES), 0).astype(F32).astype(BF)
    chunk = lax.broadcasted_iota(jnp.int32, (32, LANES), 0).astype(F32).astype(BF)
    one, zero = jnp.ones((LANES, LANES), BF), jnp.zeros((LANES, LANES), BF)
    none = jnp.zeros((32, LANES), BF)
    tail = WIN - LANES

    def rows_of(row, count):
        part = jnp.broadcast_to(row, (16, LANES)).astype(BF)
        return jnp.concatenate([part] * (count // 16), axis=0)

    def product(places, scores):
        low = (places & (LANES - 1)).astype(F32)
        high = (places >> 7).astype(F32)
        left, right = [], []
        for n in range(places.shape[0]):
            right.append(jnp.where(which == rows_of(low[n : n + 1], LANES), one, zero))
            here = chunk == rows_of(high[n : n + 1], 32)
            parts = [jnp.where(here, rows_of(score[n : n + 1], 32), none) for score in scores]
            left.append(jnp.concatenate(parts, axis=0))
        return nt(jnp.concatenate(left, axis=1), jnp.concatenate(right, axis=1))

    place_ref[...] = jnp.zeros_like(place_ref)
    rest_ref[...] = jnp.zeros_like(rest_ref)
    place_ref[:, :WIN] = pos_ref[:, LANES:].T
    for h in range(HEADS):
        rest_ref[h, :, :WIN] = score_ref[h, :, LANES:].T
    total = jnp.zeros((HEADS * 32, LANES), F32)
    for k in range(2):
        for at in range(0, tail, min(tail,16)):
            lanes = slice(k * LANES, (k + 1) * LANES)
            rows = slice(at, at + min(tail,16))
            total += product(place_ref[rows, lanes], [rest_ref[h, rows, lanes] for h in range(HEADS)])
    for at in range(0, WIN, 16):
        rows = slice(at, at + 16)
        total += product(pos_ref[rows, :LANES], [score_ref[h, rows, :LANES] for h in range(HEADS)])
    table_ref[...] = total


def block_kernel(
    region_ref, core_ref, x_ref, g_ref, earth_ref, gains_ref, qkv_ref, proj_ref, up_ref, down_ref,
    grad_ref, send_ref, keep_ref, score_ref, triple_ref, wide_ref, gain_ref,
):
    scale = SIZE ** (-0.5)
    x = x_ref[...].astype(F32)
    g_low = g_ref[...]
    gain_a, gain_b = gains_ref[0:1, :], gains_ref[1:2, :]
    normed_one, recip_one, scaled_one = layer_norm(x, gain_a)
    hidden_one = scaled_one.astype(BF)
    triple = nn(hidden_one, qkv_ref[...]).astype(BF)
    head_of = lax.broadcasted_iota(jnp.int32, (1, WIDTH), 1) // SIZE
    masks = [(head_of == h) for h in range(HEADS)]

    def stacked(part):
        return jnp.concatenate([jnp.where(m, part, jnp.zeros_like(part)) for m in masks], axis=0)

    def joined(full):
        full = full.reshape(HEADS, WIN, WIDTH)
        total = jnp.where(masks[0], full[0], 0.0)
        for h in range(1, HEADS):
            total = jnp.where(masks[h], full[h], total)
        return total

    kept = []
    earth = earth_ref[...]
    group_row = lax.broadcasted_iota(jnp.int32, (1, WIN), 1) // WIN_LON
    group_col = lax.broadcasted_iota(jnp.int32, (WIN, 1), 0) // WIN_LON
    attended = []
    for w in range(2):
        rows = slice(w * WIN, (w + 1) * WIN)
        part = triple[rows]
        query, keys, vals = part[:, :WIDTH], part[:, WIDTH : 2 * WIDTH], part[:, 2 * WIDTH :]
        label_row = jnp.zeros((1, WIN), jnp.int32)
        label_col = jnp.zeros((WIN, 1), jnp.int32)
        for group in range(WIN_PL * WIN_LAT):
            label = region_ref[group % WIN_LAT, w * WIN_PL + group // WIN_LAT]
            label_row = jnp.where(group_row == group, label, label_row)
            label_col = jnp.where(group_col == group, label, label_col)
        same = label_row == label_col
        q_stack = stacked(query)
        scores = nt(q_stack, keys).reshape(HEADS, WIN, WIN) * scale + earth
        expo = jnp.where(same[None], jnp.exp(scores), 0.0)
        probs = expo / jnp.sum(expo, axis=-1, keepdims=True)
        probs_low = probs.astype(BF).reshape(HEADS * WIN, WIN)
        attended.append(joined(nn(probs_low, vals)).astype(BF))
        kept.append((q_stack, keys, vals, probs, probs_low))
    attended = jnp.concatenate(attended, axis=0)

    resid = (x + nn(attended, proj_ref[...])).astype(BF)
    normed_two, recip_two, scaled_two = layer_norm(resid.astype(F32), gain_b)
    hidden_two = scaled_two.astype(BF)
    acted, slope = gelu_parts(nn(hidden_two, up_ref[...]))
    acted_low = acted.astype(BF)
    down = tn(g_low, acted_low)
    grad_act = (nn(g_low, down_ref[...]) * slope).astype(BF)
    up = tn(hidden_two, grad_act)
    grad_hid_two = nt(grad_act, up_ref[...])
    gain_ref[...] = jnp.zeros_like(gain_ref)
    gain = jnp.sum(grad_hid_two * normed_two, axis=0, keepdims=True)
    gain_ref[2:3, :] = gain[:, :LANES]
    gain_ref[3:4, : WIDTH - LANES] = gain[:, LANES:]
    grad_resid = (
        g_low.astype(F32) + norm_back(grad_hid_two, normed_two, recip_two, gain_b)
    ).astype(BF)
    wide_ref[:, 3 * WIDTH :] = tn(attended, grad_resid)
    grad_att = nt(grad_resid, proj_ref[...]).astype(BF)
    total = None
    for w in range(2):
        rows = slice(w * WIN, (w + 1) * WIN)
        q_stack, keys, vals, probs, probs_low = kept[w]
        a_stack = stacked(grad_att[rows])
        grad_prob = nt(a_stack, vals).reshape(HEADS, WIN, WIN)
        grad_score = probs * (grad_prob - jnp.sum(probs * grad_prob, axis=-1, keepdims=True))
        total = grad_score if total is None else total + grad_score
        grad_low = (grad_score * scale).astype(BF).reshape(HEADS * WIN, WIN)
        triple_ref[rows, :WIDTH] = joined(nn(grad_low, keys)).astype(BF)
        triple_ref[rows, WIDTH : 2 * WIDTH] = tn(grad_low, q_stack).astype(BF)
        triple_ref[rows, 2 * WIDTH :] = tn(probs_low, a_stack).astype(BF)
    score_ref[...] = total
    grad_triple = triple_ref[...]
    wide_ref[:, : 3 * WIDTH] = tn(hidden_one, grad_triple)
    grad_hid_one = nt(grad_triple, qkv_ref[...])
    gain = jnp.sum(grad_hid_one * normed_one, axis=0, keepdims=True)
    gain_ref[0:1, :] = gain[:, :LANES]
    gain_ref[1:2, : WIDTH - LANES] = gain[:, LANES:]
    grad_ref[...] = (
        grad_resid.astype(F32) + norm_back(grad_hid_one, normed_one, recip_one, gain_a)
    ).astype(BF)
    lines = {}
    for part, whole in enumerate((wide_ref[...], up, down)):
        for k in range(6):
            lines[part * 6 + k] = whole[:, k * LANES : (k + 1) * LANES].astype(BF)
    extra = [jnp.zeros((HALF - 9 * WIDTH, LANES), BF), gain_ref[...].astype(BF)]

    def put(ref, half):
        for k in range(9):
            ref[k * WIDTH : (k + 1) * WIDTH, :] = lines[half * 9 + k]
        ref[9 * WIDTH :, :] = extra[half]

    core = core_ref[0]
    for mine in range(2):

        @pl.when(core == mine)
        def _():
            put(keep_ref, mine)
            put(send_ref, 1 - mine)


def first_sum_kernel(keep_ref, came_ref, table_ref, out_ref, total_ref, pad_ref):
    total_ref[...] = keep_ref[...].astype(F32) + came_ref[...].astype(F32)
    pad_ref[...] = jnp.zeros_like(pad_ref)
    for p in range(NEAR):
        pad_ref[p, :PIECE, :] = total_ref[p * PIECE : (p + 1) * PIECE, :]
        pad_ref[p, PIECE : PIECE + BIAS_PIECE, :] = table_ref[p * BIAS_PIECE : (p + 1) * BIAS_PIECE, :]
    out_ref[...] = pad_ref[...].astype(BF)


def second_sum_kernel(came_ref, out_ref, line_ref):
    came = came_ref[...].astype(F32)
    line_ref[:PIECE, :] = jnp.sum(came[:, :PIECE], axis=0)
    table = came[:, PIECE:].reshape(NEAR // Y // 2, Y, 2, 8, LANES)
    table = jnp.sum(jnp.sum(table, axis=2), axis=0)
    for y in range(Y):
        at = PIECE + y * BIAS_PIECE
        line_ref[at : at + BIAS_PIECE, :] = table[y, :BIAS_PIECE]
    line = line_ref[...].astype(BF)
    for n in range(FAR):
        out_ref[n] = line


def fan_kernel(came_ref, *refs):
    out_ref, line_ref, pad_ref = refs[-3:]
    line_ref[...] = jnp.sum(came_ref[...].astype(F32), axis=0)
    pad_ref[...] = jnp.zeros_like(pad_ref)
    for y in range(Y):
        at = PIECE + y * BIAS_PIECE
        pad_ref[y, :PIECE, :] = line_ref[:PIECE, :]
        pad_ref[y, PIECE : PIECE + BIAS_PIECE, :] = line_ref[at : at + BIAS_PIECE, :]
    pieces = pad_ref[...].astype(BF)
    for p in range(NEAR):
        out_ref[p] = pieces[p // 2 % Y]


def finish_kernel(
    factor, core_ref, mine_ref, came_ref, qkv_out, proj_out, up_out, down_out, gains_ref, bias_ref,
    flat_ref, wide_ref, qkv_ref, proj_ref, up_ref, down_ref, done,
):
    core = core_ref[0]
    mine, came = mine_ref[...].astype(F32), came_ref[...].astype(F32)
    for p in range(NEAR):
        rows = slice(p * PIECE, (p + 1) * PIECE)
        flat_ref[core, rows, :] = mine[p, :PIECE] * factor
        flat_ref[1 - core, rows, :] = came[p, :PIECE] * factor

    def block(k):
        rows = slice(k % 9 * WIDTH, (k % 9 + 1) * WIDTH)
        return flat_ref[k // 9, rows, :]

    def leave(n, ref, out):
        copy = pltpu.make_async_copy(ref, out, done.at[n])
        copy.start()
        return copy

    for k in range(6):
        up_ref[:, k * LANES : (k + 1) * LANES] = block(6 + k)
    copies = [leave(0, up_ref, up_out)]
    for k in range(6):
        down_ref[:, k * LANES : (k + 1) * LANES] = block(12 + k)
    copies.append(leave(1, down_ref, down_out))
    for k in range(6):
        wide_ref[:, k * LANES : (k + 1) * LANES] = block(k)
    qkv_ref[...] = wide_ref[:, : 3 * WIDTH]
    copies.append(leave(2, qkv_ref, qkv_out))
    proj_ref[...] = wide_ref[:, 3 * WIDTH :]
    copies.append(leave(3, proj_ref, proj_out))
    gains = flat_ref[1, 9 * WIDTH :, :]
    for n in range(2):
        gains_ref[n : n + 1, :LANES] = gains[2 * n : 2 * n + 1]
        gains_ref[n : n + 1, LANES:] = gains[2 * n + 1 : 2 * n + 2, : WIDTH - LANES]
    for p in range(NEAR):
        piece = mine[p, PIECE:]
        for r in range(BIAS_PIECE):
            h, c = divmod(p * BIAS_PIECE + r, 32)
            width = min(LANES, BIAS_POS - c * LANES)
            if width > 0:
                bias_ref[h, :, c * LANES : c * LANES + width] = piece[r : r + 1, :width]
    for copy in copies:
        copy.wait()


VMEM = pl.BlockSpec(memory_space=pltpu.VMEM)
SMEM = pl.BlockSpec(memory_space=pltpu.SMEM)
ANY = pl.BlockSpec(memory_space=pl.ANY)


def kernel(function, name, outs, scratch=(), copies=0, scalars=0, later=0, outside=0, flops=1_000_000, moved=1_000_000):
    shapes = tuple(jax.ShapeDtypeStruct(s, t) for s, t in outs)

    def call(*args):
        return pl.pallas_call(
            function,
            out_shape=shapes,
            in_specs=[SMEM] * scalars + [VMEM] * (len(args) - scalars - later) + [ANY] * later,
            out_specs=(ANY,) * outside + (VMEM,) * (len(shapes) - outside),
            scratch_shapes=[pltpu.VMEM(s, t) for s, t in scratch] + [pltpu.SemaphoreType.DMA((copies,))] * (copies > 0),
            compiler_params=pltpu.CompilerParams(vmem_limit_bytes=48 * 1024 * 1024),
            cost_estimate=pl.CostEstimate(flops=flops, bytes_accessed=moved, transcendentals=0),
            name=name,
        )(*args)

    return call


REST = [((WIN - LANES, 2 * LANES), jnp.int32), ((HEADS, WIN - LANES, 2 * LANES), F32)]
find_bias = kernel(bias_kernel, "find_bias", [((HEADS, WIN, WIN), F32)], REST + [((8, CHUNKS * LANES), jnp.int32)], later=5, flops=20_000_000)
spread_bias = kernel(
    scatter_kernel,
    "spread_bias",
    [((HEADS * 32, LANES), F32)],
    REST,
    flops=1_000_000_000,
)
block_grads = kernel(
    block_kernel,
    "block_grads",
    [((CELLS, WIDTH), BF), ((HALF, LANES), BF), ((HALF, LANES), BF), ((HEADS, WIN, WIN), F32)],
    [((CELLS, 3 * WIDTH), BF), ((WIDTH, 4 * WIDTH), F32), ((HALF - 9 * WIDTH, LANES), F32)],
    scalars=2,
    flops=1_000_000_000,
    moved=4_000_000,
)
first_sum = kernel(
    first_sum_kernel, "first_sum", [((NEAR, 64, LANES), BF)], [((HALF, LANES), F32), ((NEAR, 64, LANES), F32)]
)
second_sum = kernel(
    second_sum_kernel, "second_sum", [((FAR, LINE, LANES), BF)], [((LINE, LANES), F32)]
)
fan = kernel(
    fan_kernel, "fan", [((NEAR, 64, LANES), BF)], [((LINE, LANES), F32), ((Y, 64, LANES), F32)], later=3
)


def finish(factor, core, mine, came):
    return kernel(
        lambda *refs: finish_kernel(factor, *refs),
        "finish",
        [
            ((WIDTH, 3 * WIDTH), F32),
            ((WIDTH, WIDTH), F32),
            ((WIDTH, 4 * WIDTH), F32),
            ((WIDTH, 4 * WIDTH), F32),
            ((2, WIDTH), F32),
            ((HEADS, 1, BIAS_POS), F32),
        ],
        [((2, HALF, LANES), F32), ((WIDTH, 4 * WIDTH), F32)]
        + [((WIDTH, 3 * WIDTH), F32), ((WIDTH, WIDTH), F32), ((WIDTH, 4 * WIDTH), F32), ((WIDTH, 4 * WIDTH), F32)],
        copies=4,
        scalars=1,
        outside=4,
    )(core, mine, came)


def routes(lon_step, lat_step):
    lon, lat, mem = 2 * Z, 2 * Y, 2
    return [
        ((a * lat + b) * mem + c, ((a + lon_step) % lon * lat + (b + lat_step) % lat) * mem + c)
        for a in range(lon)
        for b in range(lat)
        for c in range(mem)
    ]


def shifted(pair):
    half_rows, half_cols = pair.shape[2] // 2, pair.shape[3] // 2
    pair = jnp.roll(pair, -1, axis=1)
    own, east = pair[:, :, half_rows:, half_cols:], pair[:, :, half_rows:, :half_cols]
    south, corner = pair[:, :, :half_rows, half_cols:], pair[:, :, :half_rows, :half_cols]
    corner = lax.ppermute(corner, ALL, routes(-1, -1))
    east = lax.ppermute(east, ALL, routes(-1, 0))
    south = lax.ppermute(south, ALL, routes(0, -1))
    top = jnp.concatenate([own, east], axis=3)
    bottom = jnp.concatenate([south, corner], axis=3)
    return jnp.concatenate([top, bottom], axis=2)


def sent_back(grad):
    half_rows, half_cols = grad.shape[1] // 2, grad.shape[2] // 2
    east, south = grad[:, :half_rows, half_cols:], grad[:, half_rows:, :half_cols]
    corner = grad[:, half_rows:, half_cols:]
    corner = lax.ppermute(corner, ALL, routes(1, 1))
    east = lax.ppermute(east, ALL, routes(1, 0))
    south = lax.ppermute(south, ALL, routes(0, 1))
    return corner, east, south


def unshifted(grad, corner, east, south):
    own = grad[:, : grad.shape[1] // 2, : grad.shape[2] // 2]
    top = jnp.concatenate([corner, south], axis=2)
    bottom = jnp.concatenate([east, own], axis=2)
    return jnp.roll(jnp.concatenate([top, bottom], axis=1), 1, axis=0)


def body(states, cotangent, region, pos_index, w_qkv, w_proj, w_up, w_down, gains, earth_bias):
    levels, rows, merged = states.shape[1:]
    weights = (gains, w_qkv, w_proj, w_up, w_down.T)
    (earth,) = find_bias(pos_index, earth_bias.transpose(1, 0, 2), *weights)
    pair = shifted(jnp.concatenate([states, cotangent], axis=0))
    cells = pair.reshape(2, CELLS, WIDTH)
    core = lax.axis_index("c").astype(jnp.int32).reshape(1)
    grad, send, keep, score = block_grads(
        region, core, cells[0], cells[1], earth, *weights
    )
    came = lax.ppermute(send, "c", SWAP)
    grad = grad.reshape(levels, rows, merged)
    back = sent_back(grad)
    (spread,) = spread_bias(pos_index, score)
    (plane,) = first_sum(keep, came, spread)
    plane = lax.all_to_all(plane, PLANE, 0, 0)
    (line,) = second_sum(plane)
    line = lax.all_to_all(line, "far", 0, 0)
    (plane,) = fan(line, *back)
    plane = lax.all_to_all(plane, PLANE, 0, 0)
    came = lax.ppermute(plane, "c", SWAP)
    factor = float(CELLS * lax.axis_size(ALL)) ** (-0.5)
    grad_qkv, grad_proj, grad_up, grad_down, grad_gains, grad_bias = finish(factor, core, plane, came)
    grad_states = unshifted(grad, *back)[None]
    return (grad_states, grad_qkv, grad_proj, grad_up, grad_down.T, grad_gains, grad_bias.transpose(1, 0, 2))


def solution(mesh):
    fine = Mesh(mesh.devices.reshape(2, FAR, 2, Y, 2, 2), ALL)
    lon, lat = ("x", "far", "pair"), ("y", "c")
    return jax.shard_map(
        body,
        mesh=fine,
        in_specs=(
            P("m", None, lat, lon),
            P("m", None, lat, lon),
            P(lat, None),
            P(),
            P(),
            P(),
            P(),
            P(),
            P(),
            P(lat, None, None),
        ),
        out_specs=(P("m", None, lat, lon), P(), P(), P(), P(), P(), P(lat, None, None)),
        check_vma=False,
    )
```

```python
import jax
import jax.numpy as jnp
from jax import lax
from jax.experimental import pallas as pl
from jax.experimental.pallas import tpu as pltpu
from jax.sharding import Mesh
from jax.sharding import PartitionSpec as P

HEADS = 6
SIZE = 32
WIDTH = 192
WIN = 144
CELLS = 288
WIN_PL = 2
WIN_LAT = 6
WIN_LON = 12
BIAS_POS = 3312
CHUNKS = 26
LANES = 128
EPS = 1e-05
Y, Z, FAR = 4, 16, 8
NEAR = 32
HALF = 1792
PIECE = HALF // NEAR
BIAS_PIECE = HEADS * 32 // NEAR
LINE = PIECE + Y * BIAS_PIECE
ALL = ("x", "far", "pair", "y", "c", "m")
PLANE = ("x", "m", "y", "pair")
SWAP = [(0, 1), (1, 0)]
BF = jnp.bfloat16
F32 = jnp.float32


def nn(left, right):
    return lax.dot_general(left, right, (((1,), (0,)), ((), ())), preferred_element_type=F32)


def nt(left, right):
    return lax.dot_general(left, right, (((1,), (1,)), ((), ())), preferred_element_type=F32)


def tn(left, right):
    return lax.dot_general(left, right, (((0,), (0,)), ((), ())), preferred_element_type=F32)


def layer_norm(source, gain):
    centre = source - jnp.mean(source, axis=-1, keepdims=True)
    recip = lax.rsqrt(jnp.mean(centre * centre, axis=-1, keepdims=True) + EPS)
    normed = centre * recip
    return (normed, recip, normed * gain)


def norm_back(upper, normed, recip, gain):
    lowered = upper * gain
    return recip * (
        lowered
        - jnp.mean(lowered, axis=-1, keepdims=True)
        - normed * jnp.mean(lowered * normed, axis=-1, keepdims=True)
    )


def gelu_parts(upward):
    cumulative = 0.5 * (1.0 + lax.erf(upward * 0.7071067811865476))
    density = jnp.exp(-0.5 * upward * upward) * 0.3989422804014327
    return (upward * cumulative, cumulative + upward * density)


def bias_kernel(pos_ref, table_ref, gains_far, region_far, *refs):
    earth_ref, gains_ref, region_ref, place_ref, rest_ref, pair_ref, arrived = refs[-7:]
    fetched = [
        pltpu.make_async_copy(far, near, arrived.at[n])
        for n, (far, near) in enumerate(((gains_far, gains_ref), (region_far, region_ref)))
    ]
    for copy in fetched:
        copy.start()
    tail = WIN - LANES
    pair_ref[...] = jnp.zeros_like(pair_ref)
    for n in range(HEADS // 2):
        first, second = [
            jnp.floor(table_ref[h] * 8191.0 + 0.5).astype(jnp.int32) for h in (2 * n, 2 * n + 1)
        ]
        pair_ref[n : n + 1, :BIAS_POS] = (first << 16) + (second & 65535)

    def looked_up(place):
        low = place & (LANES - 1)
        high = place >> 7
        found = [jnp.zeros((8, LANES), jnp.int32) for _ in range(HEADS // 2)]
        for c in range(CHUNKS):
            here = high == c
            for n in range(HEADS // 2):
                row = jnp.broadcast_to(pair_ref[n : n + 1, c * LANES : (c + 1) * LANES], (8, LANES))
                taken = jnp.take_along_axis(row, low, axis=1, mode="promise_in_bounds")
                found[n] = jnp.where(here, taken, found[n])
        parts = []
        for both in found:
            parts += [both >> 16, (both << 16) >> 16]
        return [part.astype(F32) * (1.0 / 8191.0) for part in parts]

    def eight_rows(r, carry):
        rows = pl.ds(pl.multiple_of(r * 8, 8), 8)
        found = looked_up(pos_ref[rows, :LANES])
        for h in range(HEADS):
            earth_ref[h, rows, :LANES] = found[h]
        return carry

    lax.fori_loop(0, WIN // 8, eight_rows, 0, unroll=2)
    place_ref[...] = jnp.zeros_like(place_ref)
    place_ref[:, :WIN] = pos_ref[:, LANES:].T
    for at in range(0, tail, 8):
        for k in range(2):
            lanes = slice(k * LANES, (k + 1) * LANES)
            found = looked_up(place_ref[at : at + 8, lanes])
            for h in range(HEADS):
                rest_ref[h, at : at + 8, lanes] = found[h]
    for h in range(HEADS):
        earth_ref[h, :, LANES:] = rest_ref[h, :, :WIN].T
    for copy in fetched:
        copy.wait()


def scatter_kernel(pos_ref, score_ref, table_ref, place_ref, rest_ref):
    which = lax.broadcasted_iota(jnp.int32, (LANES, LANES), 0).astype(F32).astype(BF)
    chunk = lax.broadcasted_iota(jnp.int32, (32, LANES), 0).astype(F32).astype(BF)
    one, zero = jnp.ones((LANES, LANES), BF), jnp.zeros((LANES, LANES), BF)
    none = jnp.zeros((32, LANES), BF)
    tail = WIN - LANES

    def rows_of(row, count):
        part = jnp.broadcast_to(row, (16, LANES)).astype(BF)
        return jnp.concatenate([part] * (count // 16), axis=0)

    def product(places, scores):
        low = (places & (LANES - 1)).astype(F32)
        high = (places >> 7).astype(F32)
        left, right = [], []
        for n in range(places.shape[0]):
            right.append(jnp.where(which == rows_of(low[n : n + 1], LANES), one, zero))
            here = chunk == rows_of(high[n : n + 1], 32)
            parts = [jnp.where(here, rows_of(score[n : n + 1], 32), none) for score in scores]
            left.append(jnp.concatenate(parts, axis=0))
        return nt(jnp.concatenate(left, axis=1), jnp.concatenate(right, axis=1))

    place_ref[...] = jnp.zeros_like(place_ref)
    rest_ref[...] = jnp.zeros_like(rest_ref)
    place_ref[:, :WIN] = pos_ref[:, LANES:].T
    for h in range(HEADS):
        rest_ref[h, :, :WIN] = score_ref[h, :, LANES:].T
    total = jnp.zeros((HEADS * 32, LANES), F32)
    for k in range(2):
        for at in range(0, tail, min(tail,16)):
            lanes = slice(k * LANES, (k + 1) * LANES)
            rows = slice(at, at + min(tail,16))
            total += product(place_ref[rows, lanes], [rest_ref[h, rows, lanes] for h in range(HEADS)])
    for at in range(0, WIN, 16):
        rows = slice(at, at + 16)
        total += product(pos_ref[rows, :LANES], [score_ref[h, rows, :LANES] for h in range(HEADS)])
    table_ref[...] = total


def block_kernel(
    region_ref, core_ref, x_ref, g_ref, earth_ref, gains_ref, qkv_ref, proj_ref, up_ref, down_ref,
    grad_ref, send_ref, keep_ref, score_ref, triple_ref, wide_ref, gain_ref,
):
    scale = SIZE ** (-0.5)
    x = x_ref[...].astype(F32)
    g_low = g_ref[...]
    gain_a, gain_b = gains_ref[0:1, :], gains_ref[1:2, :]
    normed_one, recip_one, scaled_one = layer_norm(x, gain_a)
    hidden_one = scaled_one.astype(BF)
    triple = nn(hidden_one, qkv_ref[...]).astype(BF)
    head_of = lax.broadcasted_iota(jnp.int32, (1, WIDTH), 1) // SIZE
    masks = [(head_of == h) for h in range(HEADS)]

    def stacked(part):
        return jnp.concatenate([jnp.where(m, part, jnp.zeros_like(part)) for m in masks], axis=0)

    def joined(full):
        full = full.reshape(HEADS, WIN, WIDTH)
        total = jnp.where(masks[0], full[0], 0.0)
        for h in range(1, HEADS):
            total = jnp.where(masks[h], full[h], total)
        return total

    kept = []
    earth = earth_ref[...]
    group_row = lax.broadcasted_iota(jnp.int32, (1, WIN), 1) // WIN_LON
    group_col = lax.broadcasted_iota(jnp.int32, (WIN, 1), 0) // WIN_LON
    attended = []
    for w in range(2):
        rows = slice(w * WIN, (w + 1) * WIN)
        part = triple[rows]
        query, keys, vals = part[:, :WIDTH], part[:, WIDTH : 2 * WIDTH], part[:, 2 * WIDTH :]
        label_row = jnp.zeros((1, WIN), jnp.int32)
        label_col = jnp.zeros((WIN, 1), jnp.int32)
        for group in range(WIN_PL * WIN_LAT):
            label = region_ref[w * WIN_PL + group // WIN_LAT, group % WIN_LAT]
            label_row = jnp.where(group_row == group, label, label_row)
            label_col = jnp.where(group_col == group, label, label_col)
        same = label_row == label_col
        q_stack = stacked(query)
        scores = nt(q_stack, keys).reshape(HEADS, WIN, WIN) * scale + earth
        expo = jnp.where(same[None], jnp.exp(scores), 0.0)
        probs = expo / jnp.sum(expo, axis=-1, keepdims=True)
        probs_low = probs.astype(BF).reshape(HEADS * WIN, WIN)
        attended.append(joined(nn(probs_low, vals)).astype(BF))
        kept.append((q_stack, keys, vals, probs, probs_low))
    attended = jnp.concatenate(attended, axis=0)

    resid = (x + nn(attended, proj_ref[...])).astype(BF)
    normed_two, recip_two, scaled_two = layer_norm(resid.astype(F32), gain_b)
    hidden_two = scaled_two.astype(BF)
    acted, slope = gelu_parts(nn(hidden_two, up_ref[...]))
    acted_low = acted.astype(BF)
    down = tn(g_low, acted_low)
    grad_act = (nn(g_low, down_ref[...]) * slope).astype(BF)
    up = tn(hidden_two, grad_act)
    grad_hid_two = nt(grad_act, up_ref[...])
    gain_ref[...] = jnp.zeros_like(gain_ref)
    gain = jnp.sum(grad_hid_two * normed_two, axis=0, keepdims=True)
    gain_ref[2:3, :] = gain[:, :LANES]
    gain_ref[3:4, : WIDTH - LANES] = gain[:, LANES:]
    grad_resid = (
        g_low.astype(F32) + norm_back(grad_hid_two, normed_two, recip_two, gain_b)
    ).astype(BF)
    wide_ref[:, 3 * WIDTH :] = tn(attended, grad_resid)
    grad_att = nt(grad_resid, proj_ref[...]).astype(BF)
    total = None
    for w in range(2):
        rows = slice(w * WIN, (w + 1) * WIN)
        q_stack, keys, vals, probs, probs_low = kept[w]
        a_stack = stacked(grad_att[rows])
        grad_prob = nt(a_stack, vals).reshape(HEADS, WIN, WIN)
        grad_score = probs * (grad_prob - jnp.sum(probs * grad_prob, axis=-1, keepdims=True))
        total = grad_score if total is None else total + grad_score
        grad_low = (grad_score * scale).astype(BF).reshape(HEADS * WIN, WIN)
        triple_ref[rows, :WIDTH] = joined(nn(grad_low, keys)).astype(BF)
        triple_ref[rows, WIDTH : 2 * WIDTH] = tn(grad_low, q_stack).astype(BF)
        triple_ref[rows, 2 * WIDTH :] = tn(probs_low, a_stack).astype(BF)
    score_ref[...] = total
    grad_triple = triple_ref[...]
    wide_ref[:, : 3 * WIDTH] = tn(hidden_one, grad_triple)
    grad_hid_one = nt(grad_triple, qkv_ref[...])
    gain = jnp.sum(grad_hid_one * normed_one, axis=0, keepdims=True)
    gain_ref[0:1, :] = gain[:, :LANES]
    gain_ref[1:2, : WIDTH - LANES] = gain[:, LANES:]
    grad_ref[...] = (
        grad_resid.astype(F32) + norm_back(grad_hid_one, normed_one, recip_one, gain_a)
    ).astype(BF)
    lines = {}
    for part, whole in enumerate((wide_ref[...], up, down)):
        for k in range(6):
            lines[part * 6 + k] = whole[:, k * LANES : (k + 1) * LANES].astype(BF)
    extra = [jnp.zeros((HALF - 9 * WIDTH, LANES), BF), gain_ref[...].astype(BF)]

    def put(ref, half):
        for k in range(9):
            ref[k * WIDTH : (k + 1) * WIDTH, :] = lines[half * 9 + k]
        ref[9 * WIDTH :, :] = extra[half]

    core = core_ref[0]
    for mine in range(2):

        @pl.when(core == mine)
        def _():
            put(keep_ref, mine)
            put(send_ref, 1 - mine)


def first_sum_kernel(keep_ref, came_ref, table_ref, out_ref, total_ref, pad_ref):
    total_ref[...] = keep_ref[...].astype(F32) + came_ref[...].astype(F32)
    pad_ref[...] = jnp.zeros_like(pad_ref)
    for p in range(NEAR):
        pad_ref[p, :PIECE, :] = total_ref[p * PIECE : (p + 1) * PIECE, :]
        pad_ref[p, PIECE : PIECE + BIAS_PIECE, :] = table_ref[p * BIAS_PIECE : (p + 1) * BIAS_PIECE, :]
    out_ref[...] = pad_ref[...].astype(BF)


def second_sum_kernel(came_ref, out_ref, line_ref):
    came = came_ref[...].astype(F32)
    line_ref[:PIECE, :] = jnp.sum(came[:, :PIECE], axis=0)
    table = came[:, PIECE:].reshape(NEAR // Y // 2, Y, 2, 8, LANES)
    table = jnp.sum(jnp.sum(table, axis=2), axis=0)
    for y in range(Y):
        at = PIECE + y * BIAS_PIECE
        line_ref[at : at + BIAS_PIECE, :] = table[y, :BIAS_PIECE]
    line = line_ref[...].astype(BF)
    for n in range(FAR):
        out_ref[n] = line


def fan_kernel(came_ref, *refs):
    out_ref, line_ref, pad_ref = refs[-3:]
    line_ref[...] = jnp.sum(came_ref[...].astype(F32), axis=0)
    pad_ref[...] = jnp.zeros_like(pad_ref)
    for y in range(Y):
        at = PIECE + y * BIAS_PIECE
        pad_ref[y, :PIECE, :] = line_ref[:PIECE, :]
        pad_ref[y, PIECE : PIECE + BIAS_PIECE, :] = line_ref[at : at + BIAS_PIECE, :]
    pieces = pad_ref[...].astype(BF)
    for p in range(NEAR):
        out_ref[p] = pieces[p // 2 % Y]


def finish_kernel(
    factor, core_ref, mine_ref, came_ref, qkv_ref, proj_ref, up_ref, down_ref, gains_ref, bias_ref,
    flat_ref, wide_ref,
):
    core = core_ref[0]
    mine, came = mine_ref[...].astype(F32), came_ref[...].astype(F32)
    for p in range(NEAR):
        rows = slice(p * PIECE, (p + 1) * PIECE)
        flat_ref[core, rows, :] = mine[p, :PIECE] * factor
        flat_ref[1 - core, rows, :] = came[p, :PIECE] * factor

    def block(k):
        rows = slice(k % 9 * WIDTH, (k % 9 + 1) * WIDTH)
        return flat_ref[k // 9, rows, :]

    for k in range(6):
        lanes = slice(k * LANES, (k + 1) * LANES)
        wide_ref[:, lanes] = block(k)
        up_ref[:, lanes] = block(6 + k)
        down_ref[:, lanes] = block(12 + k)
    qkv_ref[...] = wide_ref[:, : 3 * WIDTH]
    proj_ref[...] = wide_ref[:, 3 * WIDTH :]
    gains = flat_ref[1, 9 * WIDTH :, :]
    for n in range(2):
        gains_ref[n : n + 1, :LANES] = gains[2 * n : 2 * n + 1]
        gains_ref[n : n + 1, LANES:] = gains[2 * n + 1 : 2 * n + 2, : WIDTH - LANES]
    for p in range(NEAR):
        piece = mine[p, PIECE:]
        for r in range(BIAS_PIECE):
            h, c = divmod(p * BIAS_PIECE + r, 32)
            width = min(LANES, BIAS_POS - c * LANES)
            if width > 0:
                bias_ref[h, :, c * LANES : c * LANES + width] = piece[r : r + 1, :width]


VMEM = pl.BlockSpec(memory_space=pltpu.VMEM)
SMEM = pl.BlockSpec(memory_space=pltpu.SMEM)
ANY = pl.BlockSpec(memory_space=pl.ANY)


def kernel(function, name, outs, scratch=(), scalars=0, later=0, copies=0, flops=1_000_000, moved=1_000_000):
    shapes = tuple(jax.ShapeDtypeStruct(s, t) for s, t in outs)

    def call(*args):
        return pl.pallas_call(
            function,
            out_shape=shapes,
            in_specs=[SMEM] * scalars + [VMEM] * (len(args) - scalars - later) + [ANY] * later,
            out_specs=(VMEM,) * len(shapes),
            scratch_shapes=[pltpu.VMEM(s, t) for s, t in scratch] + [pltpu.SemaphoreType.DMA((copies,))] * (copies > 0),
            compiler_params=pltpu.CompilerParams(vmem_limit_bytes=48 * 1024 * 1024),
            cost_estimate=pl.CostEstimate(flops=flops, bytes_accessed=moved, transcendentals=0),
            name=name,
        )(*args)

    return call


REST = [((WIN - LANES, 2 * LANES), jnp.int32), ((HEADS, WIN - LANES, 2 * LANES), F32)]
find_bias = kernel(
    bias_kernel,
    "find_bias",
    [((HEADS, WIN, WIN), F32), ((2, WIDTH), F32), ((4, WIN_LAT), jnp.int32)],
    REST + [((8, CHUNKS * LANES), jnp.int32)],
    copies=2,
    later=6,
    flops=20_000_000,
)
spread_bias = kernel(
    scatter_kernel,
    "spread_bias",
    [((HEADS * 32, LANES), F32)],
    REST,
    flops=1_000_000_000,
)
block_grads = kernel(
    block_kernel,
    "block_grads",
    [((CELLS, WIDTH), BF), ((HALF, LANES), BF), ((HALF, LANES), BF), ((HEADS, WIN, WIN), F32)],
    [((CELLS, 3 * WIDTH), BF), ((WIDTH, 4 * WIDTH), F32), ((HALF - 9 * WIDTH, LANES), F32)],
    scalars=2,
    flops=1_000_000_000,
    moved=4_000_000,
)
first_sum = kernel(
    first_sum_kernel, "first_sum", [((NEAR, 64, LANES), BF)], [((HALF, LANES), F32), ((NEAR, 64, LANES), F32)]
)
second_sum = kernel(
    second_sum_kernel, "second_sum", [((FAR, LINE, LANES), BF)], [((LINE, LANES), F32)]
)
fan = kernel(
    fan_kernel, "fan", [((NEAR, 64, LANES), BF)], [((LINE, LANES), F32), ((Y, 64, LANES), F32)], later=3
)


def finish(factor, core, mine, came):
    return kernel(
        lambda *refs: finish_kernel(factor, *refs),
        "finish",
        [
            ((WIDTH, 3 * WIDTH), F32),
            ((WIDTH, WIDTH), F32),
            ((WIDTH, 4 * WIDTH), F32),
            ((WIDTH, 4 * WIDTH), F32),
            ((2, WIDTH), F32),
            ((HEADS, 1, BIAS_POS), F32),
        ],
        [((2, HALF, LANES), F32), ((WIDTH, 4 * WIDTH), F32)],
        scalars=1,
    )(core, mine, came)


def routes(lon_step, lat_step):
    lon, lat, mem = 2 * Z, 2 * Y, 2
    return [
        ((a * lat + b) * mem + c, ((a + lon_step) % lon * lat + (b + lat_step) % lat) * mem + c)
        for a in range(lon)
        for b in range(lat)
        for c in range(mem)
    ]


def shifted(pair):
    half_rows, half_cols = pair.shape[2] // 2, pair.shape[3] // 2
    pair = jnp.roll(pair, -1, axis=1)
    own, east = pair[:, :, half_rows:, half_cols:], pair[:, :, half_rows:, :half_cols]
    south, corner = pair[:, :, :half_rows, half_cols:], pair[:, :, :half_rows, :half_cols]
    corner = lax.ppermute(corner, ALL, routes(-1, -1))
    east = lax.ppermute(east, ALL, routes(-1, 0))
    south = lax.ppermute(south, ALL, routes(0, -1))
    top = jnp.concatenate([own, east], axis=3)
    bottom = jnp.concatenate([south, corner], axis=3)
    return jnp.concatenate([top, bottom], axis=2)


def sent_back(grad):
    half_rows, half_cols = grad.shape[1] // 2, grad.shape[2] // 2
    east, south = grad[:, :half_rows, half_cols:], grad[:, half_rows:, :half_cols]
    corner = grad[:, half_rows:, half_cols:]
    corner = lax.ppermute(corner, ALL, routes(1, 1))
    east = lax.ppermute(east, ALL, routes(1, 0))
    south = lax.ppermute(south, ALL, routes(0, 1))
    return corner, east, south


def unshifted(grad, corner, east, south):
    own = grad[:, : grad.shape[1] // 2, : grad.shape[2] // 2]
    top = jnp.concatenate([corner, south], axis=2)
    bottom = jnp.concatenate([east, own], axis=2)
    return jnp.roll(jnp.concatenate([top, bottom], axis=1), 1, axis=0)


def body(states, cotangent, region, pos_index, w_qkv, w_proj, w_up, w_down, gains, earth_bias):
    levels, rows, merged = states.shape[1:]
    weights = (w_qkv, w_proj, w_up, w_down.T)
    far = [pltpu.with_memory_space_constraint(array, pltpu.HBM) for array in (gains, region.T)]
    earth, gains, region = find_bias(pos_index, earth_bias.transpose(1, 0, 2), *far, *weights)
    pair = shifted(jnp.concatenate([states, cotangent], axis=0))
    cells = pair.reshape(2, CELLS, WIDTH)
    core = lax.axis_index("c").astype(jnp.int32).reshape(1)
    grad, send, keep, score = block_grads(
        region, core, cells[0], cells[1], earth, gains, *weights
    )
    came = lax.ppermute(send, "c", SWAP)
    grad = grad.reshape(levels, rows, merged)
    back = sent_back(grad)
    (spread,) = spread_bias(pos_index, score)
    (plane,) = first_sum(keep, came, spread)
    plane = lax.all_to_all(plane, PLANE, 0, 0)
    (line,) = second_sum(plane)
    line = lax.all_to_all(line, "far", 0, 0)
    (plane,) = fan(line, *back)
    plane = lax.all_to_all(plane, PLANE, 0, 0)
    came = lax.ppermute(plane, "c", SWAP)
    factor = float(CELLS * lax.axis_size(ALL)) ** (-0.5)
    grad_qkv, grad_proj, grad_up, grad_down, grad_gains, grad_bias = finish(factor, core, plane, came)
    grad_states = unshifted(grad, *back)[None]
    return (grad_states, grad_qkv, grad_proj, grad_up, grad_down.T, grad_gains, grad_bias.transpose(1, 0, 2))


def solution(mesh):
    fine = Mesh(mesh.devices.reshape(2, FAR, 2, Y, 2, 2), ALL)
    lon, lat = ("x", "far", "pair"), ("y", "c")
    return jax.shard_map(
        body,
        mesh=fine,
        in_specs=(
            P("m", None, lat, lon),
            P("m", None, lat, lon),
            P(lat, None),
            P(),
            P(),
            P(),
            P(),
            P(),
            P(),
            P(lat, None, None),
        ),
        out_specs=(P("m", None, lat, lon), P(), P(), P(), P(), P(), P(lat, None, None)),
        check_vma=False,
    )
```

```python
import jax
import jax.numpy as jnp
from jax import lax
from jax.experimental import pallas as pl
from jax.experimental.pallas import tpu as pltpu
from jax.sharding import Mesh
from jax.sharding import PartitionSpec as P

HEADS = 6
SIZE = 32
WIDTH = 192
WIN = 144
CELLS = 288
WIN_PL = 2
WIN_LAT = 6
WIN_LON = 12
BIAS_POS = 3312
CHUNKS = 26
LANES = 128
EPS = 1e-05
Y, Z, FAR = 4, 16, 8
NEAR = 32
HALF = 1792
PIECE = HALF // NEAR
BIAS_PIECE = HEADS * 32 // NEAR
LINE = PIECE + Y * BIAS_PIECE
ALL = ("x", "far", "pair", "y", "c", "m")
PLANE = ("x", "m", "y", "pair")
SWAP = [(0, 1), (1, 0)]
BF = jnp.bfloat16
F32 = jnp.float32


def nn(left, right):
    return lax.dot_general(left, right, (((1,), (0,)), ((), ())), preferred_element_type=F32)


def nt(left, right):
    return lax.dot_general(left, right, (((1,), (1,)), ((), ())), preferred_element_type=F32)


def tn(left, right):
    return lax.dot_general(left, right, (((0,), (0,)), ((), ())), preferred_element_type=F32)


def layer_norm(source, gain):
    centre = source - jnp.mean(source, axis=-1, keepdims=True)
    recip = lax.rsqrt(jnp.mean(centre * centre, axis=-1, keepdims=True) + EPS)
    normed = centre * recip
    return (normed, recip, normed * gain)


def norm_back(upper, normed, recip, gain):
    lowered = upper * gain
    return recip * (
        lowered
        - jnp.mean(lowered, axis=-1, keepdims=True)
        - normed * jnp.mean(lowered * normed, axis=-1, keepdims=True)
    )


def gelu_parts(upward):
    cumulative = 0.5 * (1.0 + lax.erf(upward * 0.7071067811865476))
    density = jnp.exp(-0.5 * upward * upward) * 0.3989422804014327
    return (upward * cumulative, cumulative + upward * density)


def bias_kernel(pos_ref, table_ref, gains_far, region_far, *refs):
    earth_ref, gains_ref, region_ref, place_ref, rest_ref, pair_ref, arrived = refs[-7:]
    fetched = [
        pltpu.make_async_copy(far, near, arrived.at[n])
        for n, (far, near) in enumerate(((gains_far, gains_ref), (region_far, region_ref)))
    ]
    for copy in fetched:
        copy.start()
    tail = WIN - LANES
    pair_ref[...] = jnp.zeros_like(pair_ref)
    for n in range(HEADS // 2):
        first, second = [
            jnp.floor(table_ref[h] * 8191.0 + 0.5).astype(jnp.int32) for h in (2 * n, 2 * n + 1)
        ]
        pair_ref[n : n + 1, :BIAS_POS] = (first << 16) + (second & 65535)

    def looked_up(place):
        low = place & (LANES - 1)
        high = place >> 7
        found = [jnp.zeros((8, LANES), jnp.int32) for _ in range(HEADS // 2)]
        for c in range(CHUNKS):
            here = high == c
            for n in range(HEADS // 2):
                row = jnp.broadcast_to(pair_ref[n : n + 1, c * LANES : (c + 1) * LANES], (8, LANES))
                taken = jnp.take_along_axis(row, low, axis=1, mode="promise_in_bounds")
                found[n] = jnp.where(here, taken, found[n])
        parts = []
        for both in found:
            parts += [both >> 16, (both << 16) >> 16]
        return [part.astype(F32) * (1.0 / 8191.0) for part in parts]

    def eight_rows(r, carry):
        rows = pl.ds(pl.multiple_of(r * 8, 8), 8)
        found = looked_up(pos_ref[rows, :LANES])
        for h in range(HEADS):
            earth_ref[h, rows, :LANES] = found[h]
        return carry

    lax.fori_loop(0, WIN // 8, eight_rows, 0, unroll=18)
    place_ref[...] = jnp.zeros_like(place_ref)
    place_ref[:, :WIN] = pos_ref[:, LANES:].T
    for at in range(0, tail, 8):
        for k in range(2):
            lanes = slice(k * LANES, (k + 1) * LANES)
            found = looked_up(place_ref[at : at + 8, lanes])
            for h in range(HEADS):
                rest_ref[h, at : at + 8, lanes] = found[h]
    for h in range(HEADS):
        earth_ref[h, :, LANES:] = rest_ref[h, :, :WIN].T
    for copy in fetched:
        copy.wait()


def scatter_kernel(pos_ref, score_ref, table_ref, place_ref, rest_ref):
    which = lax.broadcasted_iota(jnp.int32, (LANES, LANES), 0).astype(F32).astype(BF)
    chunk = lax.broadcasted_iota(jnp.int32, (32, LANES), 0).astype(F32).astype(BF)
    one, zero = jnp.ones((LANES, LANES), BF), jnp.zeros((LANES, LANES), BF)
    none = jnp.zeros((32, LANES), BF)
    tail = WIN - LANES

    def rows_of(row, count):
        part = jnp.broadcast_to(row, (16, LANES)).astype(BF)
        return jnp.concatenate([part] * (count // 16), axis=0)

    def product(places, scores):
        low = (places & (LANES - 1)).astype(F32)
        high = (places >> 7).astype(F32)
        left, right = [], []
        for n in range(places.shape[0]):
            right.append(jnp.where(which == rows_of(low[n : n + 1], LANES), one, zero))
            here = chunk == rows_of(high[n : n + 1], 32)
            parts = [jnp.where(here, rows_of(score[n : n + 1], 32), none) for score in scores]
            left.append(jnp.concatenate(parts, axis=0))
        return nt(jnp.concatenate(left, axis=1), jnp.concatenate(right, axis=1))

    place_ref[...] = jnp.zeros_like(place_ref)
    rest_ref[...] = jnp.zeros_like(rest_ref)
    place_ref[:, :WIN] = pos_ref[:, LANES:].T
    for h in range(HEADS):
        rest_ref[h, :, :WIN] = score_ref[h, :, LANES:].T
    total = jnp.zeros((HEADS * 32, LANES), F32)
    for k in range(2):
        for at in range(0, tail, min(tail,16)):
            lanes = slice(k * LANES, (k + 1) * LANES)
            rows = slice(at, at + min(tail,16))
            total += product(place_ref[rows, lanes], [rest_ref[h, rows, lanes] for h in range(HEADS)])
    for at in range(0, WIN, 16):
        rows = slice(at, at + 16)
        total += product(pos_ref[rows, :LANES], [score_ref[h, rows, :LANES] for h in range(HEADS)])
    table_ref[...] = total


def block_kernel(
    region_ref, core_ref, x_ref, g_ref, earth_ref, gains_ref, qkv_ref, proj_ref, up_ref, down_ref,
    grad_ref, send_ref, keep_ref, score_ref, triple_ref, wide_ref, gain_ref,
):
    scale = SIZE ** (-0.5)
    x = x_ref[...].astype(F32)
    g_low = g_ref[...]
    gain_a, gain_b = gains_ref[0:1, :], gains_ref[1:2, :]
    normed_one, recip_one, scaled_one = layer_norm(x, gain_a)
    hidden_one = scaled_one.astype(BF)
    triple = nn(hidden_one, qkv_ref[...]).astype(BF)
    head_of = lax.broadcasted_iota(jnp.int32, (1, WIDTH), 1) // SIZE
    masks = [(head_of == h) for h in range(HEADS)]

    def stacked(part):
        return jnp.concatenate([jnp.where(m, part, jnp.zeros_like(part)) for m in masks], axis=0)

    def joined(full):
        full = full.reshape(HEADS, WIN, WIDTH)
        total = jnp.where(masks[0], full[0], 0.0)
        for h in range(1, HEADS):
            total = jnp.where(masks[h], full[h], total)
        return total

    kept = []
    earth = earth_ref[...]
    group_row = lax.broadcasted_iota(jnp.int32, (1, WIN), 1) // WIN_LON
    group_col = lax.broadcasted_iota(jnp.int32, (WIN, 1), 0) // WIN_LON
    attended = []
    for w in range(2):
        rows = slice(w * WIN, (w + 1) * WIN)
        part = triple[rows]
        query, keys, vals = part[:, :WIDTH], part[:, WIDTH : 2 * WIDTH], part[:, 2 * WIDTH :]
        label_row = jnp.zeros((1, WIN), jnp.int32)
        label_col = jnp.zeros((WIN, 1), jnp.int32)
        for group in range(WIN_PL * WIN_LAT):
            label = region_ref[w * WIN_PL + group // WIN_LAT, group % WIN_LAT]
            label_row = jnp.where(group_row == group, label, label_row)
            label_col = jnp.where(group_col == group, label, label_col)
        same = label_row == label_col
        q_stack = stacked(query)
        scores = nt(q_stack, keys).reshape(HEADS, WIN, WIN) * scale + earth
        expo = jnp.where(same[None], jnp.exp(scores), 0.0)
        probs = expo / jnp.sum(expo, axis=-1, keepdims=True)
        probs_low = probs.astype(BF).reshape(HEADS * WIN, WIN)
        attended.append(joined(nn(probs_low, vals)).astype(BF))
        kept.append((q_stack, keys, vals, probs, probs_low))
    attended = jnp.concatenate(attended, axis=0)

    resid = (x + nn(attended, proj_ref[...])).astype(BF)
    normed_two, recip_two, scaled_two = layer_norm(resid.astype(F32), gain_b)
    hidden_two = scaled_two.astype(BF)
    acted, slope = gelu_parts(nn(hidden_two, up_ref[...]))
    acted_low = acted.astype(BF)
    down = tn(g_low, acted_low)
    grad_act = (nn(g_low, down_ref[...]) * slope).astype(BF)
    up = tn(hidden_two, grad_act)
    grad_hid_two = nt(grad_act, up_ref[...])
    gain_ref[...] = jnp.zeros_like(gain_ref)
    gain = jnp.sum(grad_hid_two * normed_two, axis=0, keepdims=True)
    gain_ref[2:3, :] = gain[:, :LANES]
    gain_ref[3:4, : WIDTH - LANES] = gain[:, LANES:]
    grad_resid = (
        g_low.astype(F32) + norm_back(grad_hid_two, normed_two, recip_two, gain_b)
    ).astype(BF)
    wide_ref[:, 3 * WIDTH :] = tn(attended, grad_resid)
    grad_att = nt(grad_resid, proj_ref[...]).astype(BF)
    total = None
    for w in range(2):
        rows = slice(w * WIN, (w + 1) * WIN)
        q_stack, keys, vals, probs, probs_low = kept[w]
        a_stack = stacked(grad_att[rows])
        grad_prob = nt(a_stack, vals).reshape(HEADS, WIN, WIN)
        grad_score = probs * (grad_prob - jnp.sum(probs * grad_prob, axis=-1, keepdims=True))
        total = grad_score if total is None else total + grad_score
        grad_low = (grad_score * scale).astype(BF).reshape(HEADS * WIN, WIN)
        triple_ref[rows, :WIDTH] = joined(nn(grad_low, keys)).astype(BF)
        triple_ref[rows, WIDTH : 2 * WIDTH] = tn(grad_low, q_stack).astype(BF)
        triple_ref[rows, 2 * WIDTH :] = tn(probs_low, a_stack).astype(BF)
    score_ref[...] = total
    grad_triple = triple_ref[...]
    wide_ref[:, : 3 * WIDTH] = tn(hidden_one, grad_triple)
    grad_hid_one = nt(grad_triple, qkv_ref[...])
    gain = jnp.sum(grad_hid_one * normed_one, axis=0, keepdims=True)
    gain_ref[0:1, :] = gain[:, :LANES]
    gain_ref[1:2, : WIDTH - LANES] = gain[:, LANES:]
    grad_ref[...] = (
        grad_resid.astype(F32) + norm_back(grad_hid_one, normed_one, recip_one, gain_a)
    ).astype(BF)
    lines = {}
    for part, whole in enumerate((wide_ref[...], up, down)):
        for k in range(6):
            lines[part * 6 + k] = whole[:, k * LANES : (k + 1) * LANES].astype(BF)
    extra = [jnp.zeros((HALF - 9 * WIDTH, LANES), BF), gain_ref[...].astype(BF)]

    def put(ref, half):
        for k in range(9):
            ref[k * WIDTH : (k + 1) * WIDTH, :] = lines[half * 9 + k]
        ref[9 * WIDTH :, :] = extra[half]

    core = core_ref[0]
    for mine in range(2):

        @pl.when(core == mine)
        def _():
            put(keep_ref, mine)
            put(send_ref, 1 - mine)


def first_sum_kernel(keep_ref, came_ref, table_ref, out_ref, total_ref, pad_ref):
    total_ref[...] = keep_ref[...].astype(F32) + came_ref[...].astype(F32)
    pad_ref[...] = jnp.zeros_like(pad_ref)
    for p in range(NEAR):
        pad_ref[p, :PIECE, :] = total_ref[p * PIECE : (p + 1) * PIECE, :]
        pad_ref[p, PIECE : PIECE + BIAS_PIECE, :] = table_ref[p * BIAS_PIECE : (p + 1) * BIAS_PIECE, :]
    out_ref[...] = pad_ref[...].astype(BF)


def second_sum_kernel(came_ref, out_ref, line_ref):
    came = came_ref[...].astype(F32)
    line_ref[:PIECE, :] = jnp.sum(came[:, :PIECE], axis=0)
    table = came[:, PIECE:].reshape(NEAR // Y // 2, Y, 2, 8, LANES)
    table = jnp.sum(jnp.sum(table, axis=2), axis=0)
    for y in range(Y):
        at = PIECE + y * BIAS_PIECE
        line_ref[at : at + BIAS_PIECE, :] = table[y, :BIAS_PIECE]
    line = line_ref[...].astype(BF)
    for n in range(FAR):
        out_ref[n] = line


def fan_kernel(came_ref, *refs):
    out_ref, line_ref, pad_ref = refs[-3:]
    line_ref[...] = jnp.sum(came_ref[...].astype(F32), axis=0)
    pad_ref[...] = jnp.zeros_like(pad_ref)
    for y in range(Y):
        at = PIECE + y * BIAS_PIECE
        pad_ref[y, :PIECE, :] = line_ref[:PIECE, :]
        pad_ref[y, PIECE : PIECE + BIAS_PIECE, :] = line_ref[at : at + BIAS_PIECE, :]
    pieces = pad_ref[...].astype(BF)
    for p in range(NEAR):
        out_ref[p] = pieces[p // 2 % Y]


def finish_kernel(
    factor, core_ref, mine_ref, came_ref, qkv_ref, proj_ref, up_ref, down_ref, gains_ref, bias_ref
):
    mine, came = mine_ref[...].astype(F32), came_ref[...].astype(F32)
    first = (jnp.zeros((1, 1, 1), jnp.int32) + core_ref[0]) == 0
    halves = [jnp.where(first, mine, came) * factor, jnp.where(first, came, mine) * factor]

    def put(block, rows, lines):
        if block >= 6:
            ref, at = (up_ref, down_ref)[block // 12], block % 6 * LANES
            ref[rows, at : at + LANES] = lines
        elif block < 4:
            qkv_ref[rows, block * LANES : (block + 1) * LANES] = lines
        elif block == 4:
            qkv_ref[rows, 4 * LANES :] = lines[:, : LANES // 2]
            proj_ref[rows, : LANES // 2] = lines[:, LANES // 2 :]
        else:
            proj_ref[rows, LANES // 2 :] = lines

    for half in range(2):
        for p in range(NEAR):
            lines = halves[half][p, :PIECE]
            at = 0
            while at < PIECE and p * PIECE + at < 9 * WIDTH:
                block, row = divmod(p * PIECE + at, WIDTH)
                count = min(PIECE - at, WIDTH - row)
                put(half * 9 + block, slice(row, row + count), lines[at : at + count])
                at += count
    p, at = divmod(9 * WIDTH, PIECE)
    gains = halves[1][p, at : at + 8]
    for n in range(2):
        gains_ref[n : n + 1, :LANES] = gains[2 * n : 2 * n + 1]
        gains_ref[n : n + 1, LANES:] = gains[2 * n + 1 : 2 * n + 2, : WIDTH - LANES]
    for p in range(NEAR):
        piece = mine[p, PIECE:]
        for r in range(BIAS_PIECE):
            h, c = divmod(p * BIAS_PIECE + r, 32)
            width = min(LANES, BIAS_POS - c * LANES)
            if width > 0:
                bias_ref[h, :, c * LANES : c * LANES + width] = piece[r : r + 1, :width]


VMEM = pl.BlockSpec(memory_space=pltpu.VMEM)
SMEM = pl.BlockSpec(memory_space=pltpu.SMEM)
ANY = pl.BlockSpec(memory_space=pl.ANY)


def kernel(function, name, outs, scratch=(), scalars=0, later=0, copies=0, flops=1_000_000, moved=1_000_000):
    shapes = tuple(jax.ShapeDtypeStruct(s, t) for s, t in outs)

    def call(*args):
        return pl.pallas_call(
            function,
            out_shape=shapes,
            in_specs=[SMEM] * scalars + [VMEM] * (len(args) - scalars - later) + [ANY] * later,
            out_specs=(VMEM,) * len(shapes),
            scratch_shapes=[pltpu.VMEM(s, t) for s, t in scratch] + [pltpu.SemaphoreType.DMA((copies,))] * (copies > 0),
            compiler_params=pltpu.CompilerParams(vmem_limit_bytes=48 * 1024 * 1024),
            cost_estimate=pl.CostEstimate(flops=flops, bytes_accessed=moved, transcendentals=0),
            name=name,
        )(*args)

    return call


REST = [((WIN - LANES, 2 * LANES), jnp.int32), ((HEADS, WIN - LANES, 2 * LANES), F32)]
find_bias = kernel(
    bias_kernel,
    "find_bias",
    [((HEADS, WIN, WIN), F32), ((2, WIDTH), F32), ((4, WIN_LAT), jnp.int32)],
    REST + [((8, CHUNKS * LANES), jnp.int32)],
    copies=2,
    later=6,
    flops=20_000_000,
)
spread_bias = kernel(
    scatter_kernel,
    "spread_bias",
    [((HEADS * 32, LANES), F32)],
    REST,
    flops=1_000_000_000,
)
block_grads = kernel(
    block_kernel,
    "block_grads",
    [((CELLS, WIDTH), BF), ((HALF, LANES), BF), ((HALF, LANES), BF), ((HEADS, WIN, WIN), F32)],
    [((CELLS, 3 * WIDTH), BF), ((WIDTH, 4 * WIDTH), F32), ((HALF - 9 * WIDTH, LANES), F32)],
    scalars=2,
    flops=1_000_000_000,
    moved=4_000_000,
)
first_sum = kernel(
    first_sum_kernel, "first_sum", [((NEAR, 64, LANES), BF)], [((HALF, LANES), F32), ((NEAR, 64, LANES), F32)]
)
second_sum = kernel(
    second_sum_kernel, "second_sum", [((FAR, LINE, LANES), BF)], [((LINE, LANES), F32)]
)
fan = kernel(
    fan_kernel, "fan", [((NEAR, 64, LANES), BF)], [((LINE, LANES), F32), ((Y, 64, LANES), F32)], later=3
)


def finish(factor, core, mine, came):
    return kernel(
        lambda *refs: finish_kernel(factor, *refs),
        "finish",
        [
            ((WIDTH, 3 * WIDTH), F32),
            ((WIDTH, WIDTH), F32),
            ((WIDTH, 4 * WIDTH), F32),
            ((WIDTH, 4 * WIDTH), F32),
            ((2, WIDTH), F32),
            ((HEADS, 1, BIAS_POS), F32),
        ],
        scalars=1,
    )(core, mine, came)


def routes(lon_step, lat_step):
    lon, lat, mem = 2 * Z, 2 * Y, 2
    return [
        ((a * lat + b) * mem + c, ((a + lon_step) % lon * lat + (b + lat_step) % lat) * mem + c)
        for a in range(lon)
        for b in range(lat)
        for c in range(mem)
    ]


def shifted(pair):
    half_rows, half_cols = pair.shape[2] // 2, pair.shape[3] // 2
    pair = jnp.roll(pair, -1, axis=1)
    own, east = pair[:, :, half_rows:, half_cols:], pair[:, :, half_rows:, :half_cols]
    south, corner = pair[:, :, :half_rows, half_cols:], pair[:, :, :half_rows, :half_cols]
    corner = lax.ppermute(corner, ALL, routes(-1, -1))
    east = lax.ppermute(east, ALL, routes(-1, 0))
    south = lax.ppermute(south, ALL, routes(0, -1))
    top = jnp.concatenate([own, east], axis=3)
    bottom = jnp.concatenate([south, corner], axis=3)
    return jnp.concatenate([top, bottom], axis=2)


def sent_back(grad):
    half_rows, half_cols = grad.shape[1] // 2, grad.shape[2] // 2
    east, south = grad[:, :half_rows, half_cols:], grad[:, half_rows:, :half_cols]
    corner = grad[:, half_rows:, half_cols:]
    corner = lax.ppermute(corner, ALL, routes(1, 1))
    east = lax.ppermute(east, ALL, routes(1, 0))
    south = lax.ppermute(south, ALL, routes(0, 1))
    return corner, east, south


def unshifted(grad, corner, east, south):
    own = grad[:, : grad.shape[1] // 2, : grad.shape[2] // 2]
    top = jnp.concatenate([corner, south], axis=2)
    bottom = jnp.concatenate([east, own], axis=2)
    return jnp.roll(jnp.concatenate([top, bottom], axis=1), 1, axis=0)


def body(states, cotangent, region, pos_index, w_qkv, w_proj, w_up, w_down, gains, earth_bias):
    levels, rows, merged = states.shape[1:]
    weights = (w_qkv, w_proj, w_up, w_down.T)
    far = [pltpu.with_memory_space_constraint(array, pltpu.HBM) for array in (gains, region.T)]
    earth, gains, region = find_bias(pos_index, earth_bias.transpose(1, 0, 2), *far, *weights)
    pair = shifted(jnp.concatenate([states, cotangent], axis=0))
    cells = pair.reshape(2, CELLS, WIDTH)
    core = lax.axis_index("c").astype(jnp.int32).reshape(1)
    grad, send, keep, score = block_grads(
        region, core, cells[0], cells[1], earth, gains, *weights
    )
    came = lax.ppermute(send, "c", SWAP)
    grad = grad.reshape(levels, rows, merged)
    back = sent_back(grad)
    (spread,) = spread_bias(pos_index, score)
    (plane,) = first_sum(keep, came, spread)
    plane = lax.all_to_all(plane, PLANE, 0, 0)
    (line,) = second_sum(plane)
    line = lax.all_to_all(line, "far", 0, 0)
    (plane,) = fan(line, *back)
    plane = lax.all_to_all(plane, PLANE, 0, 0)
    came = lax.ppermute(plane, "c", SWAP)
    factor = float(CELLS * lax.axis_size(ALL)) ** (-0.5)
    grad_qkv, grad_proj, grad_up, grad_down, grad_gains, grad_bias = finish(factor, core, plane, came)
    grad_states = unshifted(grad, *back)[None]
    return (grad_states, grad_qkv, grad_proj, grad_up, grad_down.T, grad_gains, grad_bias.transpose(1, 0, 2))


def solution(mesh):
    fine = Mesh(mesh.devices.reshape(2, FAR, 2, Y, 2, 2), ALL)
    lon, lat = ("x", "far", "pair"), ("y", "c")
    return jax.shard_map(
        body,
        mesh=fine,
        in_specs=(
            P("m", None, lat, lon),
            P("m", None, lat, lon),
            P(lat, None),
            P(),
            P(),
            P(),
            P(),
            P(),
            P(),
            P(lat, None, None),
        ),
        out_specs=(P("m", None, lat, lon), P(), P(), P(), P(), P(), P(lat, None, None)),
        check_vma=False,
    )
```

```python
import jax
import jax.numpy as jnp
from jax import lax
from jax.experimental import pallas as pl
from jax.experimental.pallas import tpu as pltpu
from jax.sharding import Mesh
from jax.sharding import PartitionSpec as P

HEADS = 6
SIZE = 32
WIDTH = 192
WIN = 144
CELLS = 288
WIN_PL = 2
WIN_LAT = 6
WIN_LON = 12
BIAS_POS = 3312
CHUNKS = 26
LANES = 128
EPS = 1e-05
Y, Z, FAR = 4, 16, 8
NEAR = 32
HALF = 1792
PIECE = HALF // NEAR
BIAS_PIECE = HEADS * 32 // NEAR
LINE = PIECE + Y * BIAS_PIECE
ALL = ("x", "far", "pair", "y", "c", "m")
PLANE = ("x", "m", "y", "pair")
SWAP = [(0, 1), (1, 0)]
BF = jnp.bfloat16
F32 = jnp.float32


def nn(left, right):
    return lax.dot_general(left, right, (((1,), (0,)), ((), ())), preferred_element_type=F32)


def nt(left, right):
    return lax.dot_general(left, right, (((1,), (1,)), ((), ())), preferred_element_type=F32)


def tn(left, right):
    return lax.dot_general(left, right, (((0,), (0,)), ((), ())), preferred_element_type=F32)


def layer_norm(source, gain):
    centre = source - jnp.mean(source, axis=-1, keepdims=True)
    recip = lax.rsqrt(jnp.mean(centre * centre, axis=-1, keepdims=True) + EPS)
    normed = centre * recip
    return (normed, recip, normed * gain)


def norm_back(upper, normed, recip, gain):
    lowered = upper * gain
    return recip * (
        lowered
        - jnp.mean(lowered, axis=-1, keepdims=True)
        - normed * jnp.mean(lowered * normed, axis=-1, keepdims=True)
    )


def gelu_parts(upward):
    cumulative = 0.5 * (1.0 + lax.erf(upward * 0.7071067811865476))
    density = jnp.exp(-0.5 * upward * upward) * 0.3989422804014327
    return (upward * cumulative, cumulative + upward * density)


def bias_kernel(pos_ref, table_ref, *refs):
    (earth_ref, *near), (place_ref, rest_ref, pair_ref, arrived) = refs[6:13], refs[13:]
    fetched = [pltpu.make_async_copy(refs[n], near[n], arrived.at[n]) for n in range(6)]
    for copy in fetched:
        copy.start()
    tail = WIN - LANES
    pair_ref[...] = jnp.zeros_like(pair_ref)
    for n in range(HEADS // 2):
        first, second = [
            jnp.floor(table_ref[h] * 8191.0 + 0.5).astype(jnp.int32) for h in (2 * n, 2 * n + 1)
        ]
        pair_ref[n : n + 1, :BIAS_POS] = (first << 16) + (second & 65535)

    def looked_up(place):
        low = place & (LANES - 1)
        high = place >> 7
        found = [jnp.zeros((8, LANES), jnp.int32) for _ in range(HEADS // 2)]
        for c in range(CHUNKS):
            here = high == c
            for n in range(HEADS // 2):
                row = jnp.broadcast_to(pair_ref[n : n + 1, c * LANES : (c + 1) * LANES], (8, LANES))
                taken = jnp.take_along_axis(row, low, axis=1, mode="promise_in_bounds")
                found[n] = jnp.where(here, taken, found[n])
        parts = []
        for both in found:
            parts += [both >> 16, (both << 16) >> 16]
        return [part.astype(F32) * (1.0 / 8191.0) for part in parts]

    def eight_rows(r, carry):
        rows = pl.ds(pl.multiple_of(r * 8, 8), 8)
        found = looked_up(pos_ref[rows, :LANES])
        for h in range(HEADS):
            earth_ref[h, rows, :LANES] = found[h]
        return carry

    lax.fori_loop(0, WIN // 8, eight_rows, 0, unroll=18)
    place_ref[...] = jnp.zeros_like(place_ref)
    place_ref[:, :WIN] = pos_ref[:, LANES:].T
    for at in range(0, tail, 8):
        for k in range(2):
            lanes = slice(k * LANES, (k + 1) * LANES)
            found = looked_up(place_ref[at : at + 8, lanes])
            for h in range(HEADS):
                rest_ref[h, at : at + 8, lanes] = found[h]
    for h in range(HEADS):
        earth_ref[h, :, LANES:] = rest_ref[h, :, :WIN].T
    for copy in fetched:
        copy.wait()


def scatter_kernel(pos_ref, score_ref, table_ref, place_ref, rest_ref):
    which = lax.broadcasted_iota(jnp.int32, (LANES, LANES), 0).astype(F32).astype(BF)
    chunk = lax.broadcasted_iota(jnp.int32, (32, LANES), 0).astype(F32).astype(BF)
    one, zero = jnp.ones((LANES, LANES), BF), jnp.zeros((LANES, LANES), BF)
    none = jnp.zeros((32, LANES), BF)
    tail = WIN - LANES

    def rows_of(row, count):
        part = jnp.broadcast_to(row, (16, LANES)).astype(BF)
        return jnp.concatenate([part] * (count // 16), axis=0)

    def product(places, scores):
        low = (places & (LANES - 1)).astype(F32)
        high = (places >> 7).astype(F32)
        left, right = [], []
        for n in range(places.shape[0]):
            right.append(jnp.where(which == rows_of(low[n : n + 1], LANES), one, zero))
            here = chunk == rows_of(high[n : n + 1], 32)
            parts = [jnp.where(here, rows_of(score[n : n + 1], 32), none) for score in scores]
            left.append(jnp.concatenate(parts, axis=0))
        return nt(jnp.concatenate(left, axis=1), jnp.concatenate(right, axis=1))

    place_ref[...] = jnp.zeros_like(place_ref)
    rest_ref[...] = jnp.zeros_like(rest_ref)
    place_ref[:, :WIN] = pos_ref[:, LANES:].T
    for h in range(HEADS):
        rest_ref[h, :, :WIN] = score_ref[h, :, LANES:].T
    total = jnp.zeros((HEADS * 32, LANES), F32)
    for k in range(2):
        for at in range(0, tail, min(tail,16)):
            lanes = slice(k * LANES, (k + 1) * LANES)
            rows = slice(at, at + min(tail,16))
            total += product(place_ref[rows, lanes], [rest_ref[h, rows, lanes] for h in range(HEADS)])
    for at in range(0, WIN, 16):
        rows = slice(at, at + 16)
        total += product(pos_ref[rows, :LANES], [score_ref[h, rows, :LANES] for h in range(HEADS)])
    table_ref[...] = total


def block_kernel(
    region_ref, core_ref, cells_ref, earth_ref, gains_ref, qkv_ref, proj_ref, up_ref, down_ref,
    grad_ref, send_ref, keep_ref, score_ref, triple_ref, wide_ref, gain_ref,
):
    scale = SIZE ** (-0.5)
    level = CELLS // 4
    x, g = [
        jnp.concatenate([part[level:], part[:level]], axis=0)
        for part in (cells_ref[0].astype(F32), cells_ref[1].astype(F32))
    ]
    g_low = g.astype(BF)
    gain_a, gain_b = gains_ref[0:1, :], gains_ref[1:2, :]
    normed_one, recip_one, scaled_one = layer_norm(x, gain_a)
    hidden_one = scaled_one.astype(BF)
    triple = nn(hidden_one, qkv_ref[...]).astype(BF)
    head_of = lax.broadcasted_iota(jnp.int32, (1, WIDTH), 1) // SIZE
    masks = [(head_of == h) for h in range(HEADS)]

    def stacked(part):
        return jnp.concatenate([jnp.where(m, part, jnp.zeros_like(part)) for m in masks], axis=0)

    def joined(full):
        full = full.reshape(HEADS, WIN, WIDTH)
        total = jnp.where(masks[0], full[0], 0.0)
        for h in range(1, HEADS):
            total = jnp.where(masks[h], full[h], total)
        return total

    kept = []
    earth = earth_ref[...]
    group_row = lax.broadcasted_iota(jnp.int32, (1, WIN), 1) // WIN_LON
    group_col = lax.broadcasted_iota(jnp.int32, (WIN, 1), 0) // WIN_LON
    attended = []
    for w in range(2):
        rows = slice(w * WIN, (w + 1) * WIN)
        part = triple[rows]
        query, keys, vals = part[:, :WIDTH], part[:, WIDTH : 2 * WIDTH], part[:, 2 * WIDTH :]
        label_row = jnp.zeros((1, WIN), jnp.int32)
        label_col = jnp.zeros((WIN, 1), jnp.int32)
        for group in range(WIN_PL * WIN_LAT):
            label = region_ref[w * WIN_PL + group // WIN_LAT, group % WIN_LAT]
            label_row = jnp.where(group_row == group, label, label_row)
            label_col = jnp.where(group_col == group, label, label_col)
        same = label_row == label_col
        q_stack = stacked(query)
        scores = nt(q_stack, keys).reshape(HEADS, WIN, WIN) * scale + earth
        expo = jnp.where(same[None], jnp.exp(scores), 0.0)
        probs = expo / jnp.sum(expo, axis=-1, keepdims=True)
        probs_low = probs.astype(BF).reshape(HEADS * WIN, WIN)
        attended.append(joined(nn(probs_low, vals)).astype(BF))
        kept.append((q_stack, keys, vals, probs, probs_low))
    attended = jnp.concatenate(attended, axis=0)

    resid = (x + nn(attended, proj_ref[...])).astype(BF)
    normed_two, recip_two, scaled_two = layer_norm(resid.astype(F32), gain_b)
    hidden_two = scaled_two.astype(BF)
    acted, slope = gelu_parts(nn(hidden_two, up_ref[...]))
    acted_low = acted.astype(BF)
    down = tn(g_low, acted_low)
    grad_act = (nn(g_low, down_ref[...]) * slope).astype(BF)
    up = tn(hidden_two, grad_act)
    grad_hid_two = nt(grad_act, up_ref[...])
    gain_ref[...] = jnp.zeros_like(gain_ref)
    gain = jnp.sum(grad_hid_two * normed_two, axis=0, keepdims=True)
    gain_ref[2:3, :] = gain[:, :LANES]
    gain_ref[3:4, : WIDTH - LANES] = gain[:, LANES:]
    grad_resid = (
        g + norm_back(grad_hid_two, normed_two, recip_two, gain_b)
    ).astype(BF)
    wide_ref[:, 3 * WIDTH :] = tn(attended, grad_resid)
    grad_att = nt(grad_resid, proj_ref[...]).astype(BF)
    total = None
    for w in range(2):
        rows = slice(w * WIN, (w + 1) * WIN)
        q_stack, keys, vals, probs, probs_low = kept[w]
        a_stack = stacked(grad_att[rows])
        grad_prob = nt(a_stack, vals).reshape(HEADS, WIN, WIN)
        grad_score = probs * (grad_prob - jnp.sum(probs * grad_prob, axis=-1, keepdims=True))
        total = grad_score if total is None else total + grad_score
        grad_low = (grad_score * scale).astype(BF).reshape(HEADS * WIN, WIN)
        triple_ref[rows, :WIDTH] = joined(nn(grad_low, keys)).astype(BF)
        triple_ref[rows, WIDTH : 2 * WIDTH] = tn(grad_low, q_stack).astype(BF)
        triple_ref[rows, 2 * WIDTH :] = tn(probs_low, a_stack).astype(BF)
    score_ref[...] = total
    grad_triple = triple_ref[...]
    wide_ref[:, : 3 * WIDTH] = tn(hidden_one, grad_triple)
    grad_hid_one = nt(grad_triple, qkv_ref[...])
    gain = jnp.sum(grad_hid_one * normed_one, axis=0, keepdims=True)
    gain_ref[0:1, :] = gain[:, :LANES]
    gain_ref[1:2, : WIDTH - LANES] = gain[:, LANES:]
    grad = grad_resid.astype(F32) + norm_back(grad_hid_one, normed_one, recip_one, gain_a)
    grad_ref[...] = jnp.concatenate([grad[-level:], grad[:-level]], axis=0).astype(BF)
    lines = {}
    for part, whole in enumerate((wide_ref[...], up, down)):
        for k in range(6):
            lines[part * 6 + k] = whole[:, k * LANES : (k + 1) * LANES].astype(BF)
    extra = [jnp.zeros((HALF - 9 * WIDTH, LANES), BF), gain_ref[...].astype(BF)]

    def put(ref, half):
        for k in range(9):
            ref[k * WIDTH : (k + 1) * WIDTH, :] = lines[half * 9 + k]
        ref[9 * WIDTH :, :] = extra[half]

    core = core_ref[0]
    for mine in range(2):

        @pl.when(core == mine)
        def _():
            put(keep_ref, mine)
            put(send_ref, 1 - mine)


def first_sum_kernel(keep_ref, came_ref, table_ref, out_ref, total_ref, pad_ref):
    total_ref[...] = keep_ref[...].astype(F32) + came_ref[...].astype(F32)
    pad_ref[...] = jnp.zeros_like(pad_ref)
    for p in range(NEAR):
        pad_ref[p, :PIECE, :] = total_ref[p * PIECE : (p + 1) * PIECE, :]
        pad_ref[p, PIECE : PIECE + BIAS_PIECE, :] = table_ref[p * BIAS_PIECE : (p + 1) * BIAS_PIECE, :]
    out_ref[...] = pad_ref[...].astype(BF)


def second_sum_kernel(came_ref, out_ref, line_ref):
    came = came_ref[...].astype(F32)
    line_ref[:PIECE, :] = jnp.sum(came[:, :PIECE], axis=0)
    table = came[:, PIECE:].reshape(NEAR // Y // 2, Y, 2, 8, LANES)
    table = jnp.sum(jnp.sum(table, axis=2), axis=0)
    for y in range(Y):
        at = PIECE + y * BIAS_PIECE
        line_ref[at : at + BIAS_PIECE, :] = table[y, :BIAS_PIECE]
    line = line_ref[...].astype(BF)
    for n in range(FAR):
        out_ref[n] = line


def fan_kernel(came_ref, *refs):
    out_ref, line_ref, pad_ref = refs[-3:]
    line_ref[...] = jnp.sum(came_ref[...].astype(F32), axis=0)
    pad_ref[...] = jnp.zeros_like(pad_ref)
    for y in range(Y):
        at = PIECE + y * BIAS_PIECE
        pad_ref[y, :PIECE, :] = line_ref[:PIECE, :]
        pad_ref[y, PIECE : PIECE + BIAS_PIECE, :] = line_ref[at : at + BIAS_PIECE, :]
    pieces = pad_ref[...].astype(BF)
    for p in range(NEAR):
        out_ref[p] = pieces[p // 2 % Y]


def finish_kernel(
    factor, core_ref, mine_ref, came_ref, qkv_ref, proj_ref, up_ref, down_ref, gains_ref, bias_ref
):
    mine, came = mine_ref[...].astype(F32), came_ref[...].astype(F32)
    first = (jnp.zeros((1, 1, 1), jnp.int32) + core_ref[0]) == 0
    halves = [jnp.where(first, mine, came) * factor, jnp.where(first, came, mine) * factor]

    def put(block, rows, lines):
        if block >= 6:
            ref, at = (up_ref, down_ref)[block // 12], block % 6 * LANES
            ref[rows, at : at + LANES] = lines
        elif block < 4:
            qkv_ref[rows, block * LANES : (block + 1) * LANES] = lines
        elif block == 4:
            qkv_ref[rows, 4 * LANES :] = lines[:, : LANES // 2]
            proj_ref[rows, : LANES // 2] = lines[:, LANES // 2 :]
        else:
            proj_ref[rows, LANES // 2 :] = lines

    for half in range(2):
        for p in range(NEAR):
            lines = halves[half][p, :PIECE]
            at = 0
            while at < PIECE and p * PIECE + at < 9 * WIDTH:
                block, row = divmod(p * PIECE + at, WIDTH)
                count = min(PIECE - at, WIDTH - row)
                put(half * 9 + block, slice(row, row + count), lines[at : at + count])
                at += count
    p, at = divmod(9 * WIDTH, PIECE)
    gains = halves[1][p, at : at + 8]
    for n in range(2):
        gains_ref[n : n + 1, :LANES] = gains[2 * n : 2 * n + 1]
        gains_ref[n : n + 1, LANES:] = gains[2 * n + 1 : 2 * n + 2, : WIDTH - LANES]
    for p in range(NEAR):
        piece = mine[p, PIECE:]
        for r in range(BIAS_PIECE):
            h, c = divmod(p * BIAS_PIECE + r, 32)
            width = min(LANES, BIAS_POS - c * LANES)
            if width > 0:
                bias_ref[h, :, c * LANES : c * LANES + width] = piece[r : r + 1, :width]


VMEM = pl.BlockSpec(memory_space=pltpu.VMEM)
SMEM = pl.BlockSpec(memory_space=pltpu.SMEM)
ANY = pl.BlockSpec(memory_space=pl.ANY)


def kernel(function, name, outs, scratch=(), scalars=0, later=0, copies=0, flops=1_000_000, moved=1_000_000):
    shapes = tuple(jax.ShapeDtypeStruct(s, t) for s, t in outs)

    def call(*args):
        return pl.pallas_call(
            function,
            out_shape=shapes,
            in_specs=[SMEM] * scalars + [VMEM] * (len(args) - scalars - later) + [ANY] * later,
            out_specs=(VMEM,) * len(shapes),
            scratch_shapes=[pltpu.VMEM(s, t) for s, t in scratch] + [pltpu.SemaphoreType.DMA((copies,))] * (copies > 0),
            compiler_params=pltpu.CompilerParams(vmem_limit_bytes=48 * 1024 * 1024),
            cost_estimate=pl.CostEstimate(flops=flops, bytes_accessed=moved, transcendentals=0),
            name=name,
        )(*args)

    return call


REST = [((WIN - LANES, 2 * LANES), jnp.int32), ((HEADS, WIN - LANES, 2 * LANES), F32)]
find_bias = kernel(
    bias_kernel,
    "find_bias",
    [((HEADS, WIN, WIN), F32), ((2, WIDTH), F32), ((4, WIN_LAT), jnp.int32)]
    + [((WIDTH, 3 * WIDTH), BF), ((WIDTH, WIDTH), BF), ((WIDTH, 4 * WIDTH), BF), ((WIDTH, 4 * WIDTH), BF)],
    REST + [((8, CHUNKS * LANES), jnp.int32)],
    copies=6,
    later=6,
    flops=20_000_000,
)
spread_bias = kernel(
    scatter_kernel,
    "spread_bias",
    [((HEADS * 32, LANES), F32)],
    REST,
    flops=1_000_000_000,
)
block_grads = kernel(
    block_kernel,
    "block_grads",
    [((CELLS, WIDTH), BF), ((HALF, LANES), BF), ((HALF, LANES), BF), ((HEADS, WIN, WIN), F32)],
    [((CELLS, 3 * WIDTH), BF), ((WIDTH, 4 * WIDTH), F32), ((HALF - 9 * WIDTH, LANES), F32)],
    scalars=2,
    flops=1_000_000_000,
    moved=4_000_000,
)
first_sum = kernel(
    first_sum_kernel, "first_sum", [((NEAR, 64, LANES), BF)], [((HALF, LANES), F32), ((NEAR, 64, LANES), F32)]
)
second_sum = kernel(
    second_sum_kernel, "second_sum", [((FAR, LINE, LANES), BF)], [((LINE, LANES), F32)]
)
fan = kernel(
    fan_kernel, "fan", [((NEAR, 64, LANES), BF)], [((LINE, LANES), F32), ((Y, 64, LANES), F32)], later=3
)


def finish(factor, core, mine, came):
    return kernel(
        lambda *refs: finish_kernel(factor, *refs),
        "finish",
        [
            ((WIDTH, 3 * WIDTH), F32),
            ((WIDTH, WIDTH), F32),
            ((WIDTH, 4 * WIDTH), F32),
            ((WIDTH, 4 * WIDTH), F32),
            ((2, WIDTH), F32),
            ((HEADS, 1, BIAS_POS), F32),
        ],
        scalars=1,
    )(core, mine, came)


def routes(lon_step, lat_step):
    lon, lat, mem = 2 * Z, 2 * Y, 2
    return [
        ((a * lat + b) * mem + c, ((a + lon_step) % lon * lat + (b + lat_step) % lat) * mem + c)
        for a in range(lon)
        for b in range(lat)
        for c in range(mem)
    ]


def shifted(pair):
    half_rows, half_cols = pair.shape[2] // 2, pair.shape[3] // 2
    own, east = pair[:, :, half_rows:, half_cols:], pair[:, :, half_rows:, :half_cols]
    south, corner = pair[:, :, :half_rows, half_cols:], pair[:, :, :half_rows, :half_cols]
    corner = lax.ppermute(corner, ALL, routes(-1, -1))
    east = lax.ppermute(east, ALL, routes(-1, 0))
    south = lax.ppermute(south, ALL, routes(0, -1))
    top = jnp.concatenate([own, east], axis=3)
    bottom = jnp.concatenate([south, corner], axis=3)
    return jnp.concatenate([top, bottom], axis=2)


def sent_back(grad):
    half_rows, half_cols = grad.shape[1] // 2, grad.shape[2] // 2
    east, south = grad[:, :half_rows, half_cols:], grad[:, half_rows:, :half_cols]
    corner = grad[:, half_rows:, half_cols:]
    corner = lax.ppermute(corner, ALL, routes(1, 1))
    east = lax.ppermute(east, ALL, routes(1, 0))
    south = lax.ppermute(south, ALL, routes(0, 1))
    return corner, east, south


def unshifted(grad, corner, east, south):
    own = grad[:, : grad.shape[1] // 2, : grad.shape[2] // 2]
    top = jnp.concatenate([corner, south], axis=2)
    bottom = jnp.concatenate([east, own], axis=2)
    return jnp.concatenate([top, bottom], axis=1)


def body(states, cotangent, region, pos_index, w_qkv, w_proj, w_up, w_down, gains, earth_bias):
    levels, rows, merged = states.shape[1:]
    far = (gains, region.T, w_qkv, w_proj, w_up, w_down.T)
    far = [pltpu.with_memory_space_constraint(array, pltpu.HBM) for array in far]
    earth, gains, region, *weights = find_bias(pos_index, earth_bias.transpose(1, 0, 2), *far)
    pair = shifted(jnp.concatenate([states, cotangent], axis=0))
    cells = pair.reshape(2, CELLS, WIDTH)
    core = lax.axis_index("c").astype(jnp.int32).reshape(1)
    grad, send, keep, score = block_grads(
        region, core, cells, earth, gains, *weights
    )
    came = lax.ppermute(send, "c", SWAP)
    grad = grad.reshape(levels, rows, merged)
    back = sent_back(grad)
    (spread,) = spread_bias(pos_index, score)
    (plane,) = first_sum(keep, came, spread)
    plane = lax.all_to_all(plane, PLANE, 0, 0)
    (line,) = second_sum(plane)
    line = lax.all_to_all(line, "far", 0, 0)
    (plane,) = fan(line, *back)
    plane = lax.all_to_all(plane, PLANE, 0, 0)
    came = lax.ppermute(plane, "c", SWAP)
    factor = float(CELLS * lax.axis_size(ALL)) ** (-0.5)
    grad_qkv, grad_proj, grad_up, grad_down, grad_gains, grad_bias = finish(factor, core, plane, came)
    grad_states = unshifted(grad, *back)[None]
    return (grad_states, grad_qkv, grad_proj, grad_up, grad_down.T, grad_gains, grad_bias.transpose(1, 0, 2))


def solution(mesh):
    fine = Mesh(mesh.devices.reshape(2, FAR, 2, Y, 2, 2), ALL)
    lon, lat = ("x", "far", "pair"), ("y", "c")
    return jax.shard_map(
        body,
        mesh=fine,
        in_specs=(
            P("m", None, lat, lon),
            P("m", None, lat, lon),
            P(lat, None),
            P(),
            P(),
            P(),
            P(),
            P(),
            P(),
            P(lat, None, None),
        ),
        out_specs=(P("m", None, lat, lon), P(), P(), P(), P(), P(), P(lat, None, None)),
        check_vma=False,
    )
```

```python
import jax
import jax.numpy as jnp
from jax import lax
from jax.experimental import pallas as pl
from jax.experimental.pallas import tpu as pltpu
from jax.sharding import Mesh
from jax.sharding import PartitionSpec as P

HEADS = 6
SIZE = 32
WIDTH = 192
WIN = 144
CELLS = 288
WIN_PL = 2
WIN_LAT = 6
WIN_LON = 12
BIAS_POS = 3312
CHUNKS = 26
LANES = 128
EPS = 1e-05
Y, Z, FAR = 4, 16, 8
NEAR = 32
HALF = 1792
PIECE = HALF // NEAR
BIAS_PIECE = HEADS * 32 // NEAR
LINE = PIECE + Y * BIAS_PIECE
ALL = ("x", "far", "pair", "y", "c", "m")
PLANE = ("x", "m", "y", "pair")
SWAP = [(0, 1), (1, 0)]
BF = jnp.bfloat16
F32 = jnp.float32


def nn(left, right):
    return lax.dot_general(left, right, (((1,), (0,)), ((), ())), preferred_element_type=F32)


def nt(left, right):
    return lax.dot_general(left, right, (((1,), (1,)), ((), ())), preferred_element_type=F32)


def tn(left, right):
    return lax.dot_general(left, right, (((0,), (0,)), ((), ())), preferred_element_type=F32)


def layer_norm(source, gain):
    centre = source - jnp.mean(source, axis=-1, keepdims=True)
    recip = lax.rsqrt(jnp.mean(centre * centre, axis=-1, keepdims=True) + EPS)
    normed = centre * recip
    return (normed, recip, normed * gain)


def norm_back(upper, normed, recip, gain):
    lowered = upper * gain
    return recip * (
        lowered
        - jnp.mean(lowered, axis=-1, keepdims=True)
        - normed * jnp.mean(lowered * normed, axis=-1, keepdims=True)
    )


def gelu_parts(upward):
    cumulative = 0.5 * (1.0 + lax.erf(upward * 0.7071067811865476))
    density = jnp.exp(-0.5 * upward * upward) * 0.3989422804014327
    return (upward * cumulative, cumulative + upward * density)


def cut_kernel(states_far, cot_far, own_ref, east_ref, south_ref, corner_ref, arrived):
    copies = []
    for n, far in enumerate((states_far, cot_far)):
        rows, cols = far.shape[0] // 2, far.shape[2] // 2
        for k, ref in enumerate((corner_ref, south_ref, east_ref, own_ref)):
            at = pl.ds(k // 2 * rows, rows), slice(None), pl.ds(k % 2 * cols, cols)
            copies.append(pltpu.make_async_copy(far.at[at], ref.at[n], arrived.at[4 * n + k]))
            copies[-1].start()
    for copy in copies:
        copy.wait()


def bias_kernel(pos_ref, table_ref, *refs):
    (earth_ref, *near), (place_ref, rest_ref, pair_ref, arrived) = refs[6:13], refs[13:]
    fetched = [pltpu.make_async_copy(refs[n], near[n], arrived.at[n]) for n in range(6)]
    for copy in fetched:
        copy.start()
    tail = WIN - LANES
    pair_ref[...] = jnp.zeros_like(pair_ref)
    for n in range(HEADS // 2):
        first, second = [
            jnp.floor(table_ref[h] * 8191.0 + 0.5).astype(jnp.int32) for h in (2 * n, 2 * n + 1)
        ]
        pair_ref[n : n + 1, :BIAS_POS] = (first << 16) + (second & 65535)

    def looked_up(place):
        low = place & (LANES - 1)
        high = place >> 7
        found = [jnp.zeros((8, LANES), jnp.int32) for _ in range(HEADS // 2)]
        for c in range(CHUNKS):
            here = high == c
            for n in range(HEADS // 2):
                row = jnp.broadcast_to(pair_ref[n : n + 1, c * LANES : (c + 1) * LANES], (8, LANES))
                taken = jnp.take_along_axis(row, low, axis=1, mode="promise_in_bounds")
                found[n] = jnp.where(here, taken, found[n])
        parts = []
        for both in found:
            parts += [both >> 16, (both << 16) >> 16]
        return [part.astype(F32) * (1.0 / 8191.0) for part in parts]

    def eight_rows(r, carry):
        rows = pl.ds(pl.multiple_of(r * 8, 8), 8)
        found = looked_up(pos_ref[rows, :LANES])
        for h in range(HEADS):
            earth_ref[h, rows, :LANES] = found[h]
        return carry

    lax.fori_loop(0, WIN // 8, eight_rows, 0, unroll=18)
    place_ref[...] = jnp.zeros_like(place_ref)
    place_ref[:, :WIN] = pos_ref[:, LANES:].T
    for at in range(0, tail, 8):
        for k in range(2):
            lanes = slice(k * LANES, (k + 1) * LANES)
            found = looked_up(place_ref[at : at + 8, lanes])
            for h in range(HEADS):
                rest_ref[h, at : at + 8, lanes] = found[h]
    for h in range(HEADS):
        earth_ref[h, :, LANES:] = rest_ref[h, :, :WIN].T
    for copy in fetched:
        copy.wait()


def scatter_kernel(pos_ref, score_ref, table_ref, place_ref, rest_ref):
    which = lax.broadcasted_iota(jnp.int32, (LANES, LANES), 0).astype(F32).astype(BF)
    chunk = lax.broadcasted_iota(jnp.int32, (32, LANES), 0).astype(F32).astype(BF)
    one, zero = jnp.ones((LANES, LANES), BF), jnp.zeros((LANES, LANES), BF)
    none = jnp.zeros((32, LANES), BF)
    tail = WIN - LANES

    def rows_of(row, count):
        part = jnp.broadcast_to(row, (16, LANES)).astype(BF)
        return jnp.concatenate([part] * (count // 16), axis=0)

    def product(places, scores):
        low = (places & (LANES - 1)).astype(F32)
        high = (places >> 7).astype(F32)
        left, right = [], []
        for n in range(places.shape[0]):
            right.append(jnp.where(which == rows_of(low[n : n + 1], LANES), one, zero))
            here = chunk == rows_of(high[n : n + 1], 32)
            parts = [jnp.where(here, rows_of(score[n : n + 1], 32), none) for score in scores]
            left.append(jnp.concatenate(parts, axis=0))
        return nt(jnp.concatenate(left, axis=1), jnp.concatenate(right, axis=1))

    place_ref[...] = jnp.zeros_like(place_ref)
    rest_ref[...] = jnp.zeros_like(rest_ref)
    place_ref[:, :WIN] = pos_ref[:, LANES:].T
    for h in range(HEADS):
        rest_ref[h, :, :WIN] = score_ref[h, :, LANES:].T
    total = jnp.zeros((HEADS * 32, LANES), F32)
    for k in range(2):
        for at in range(0, tail, min(tail,16)):
            lanes = slice(k * LANES, (k + 1) * LANES)
            rows = slice(at, at + min(tail,16))
            total += product(place_ref[rows, lanes], [rest_ref[h, rows, lanes] for h in range(HEADS)])
    for at in range(0, WIN, 16):
        rows = slice(at, at + 16)
        total += product(pos_ref[rows, :LANES], [score_ref[h, rows, :LANES] for h in range(HEADS)])
    table_ref[...] = total


def block_kernel(
    region_ref, core_ref, cells_ref, earth_ref, gains_ref, qkv_ref, proj_ref, up_ref, down_ref,
    grad_ref, send_ref, keep_ref, score_ref, triple_ref, wide_ref, gain_ref,
):
    scale = SIZE ** (-0.5)
    level = CELLS // 4
    x, g = [
        jnp.concatenate([part[level:], part[:level]], axis=0)
        for part in (cells_ref[0].astype(F32), cells_ref[1].astype(F32))
    ]
    g_low = g.astype(BF)
    gain_a, gain_b = gains_ref[0:1, :], gains_ref[1:2, :]
    normed_one, recip_one, scaled_one = layer_norm(x, gain_a)
    hidden_one = scaled_one.astype(BF)
    triple = nn(hidden_one, qkv_ref[...]).astype(BF)
    head_of = lax.broadcasted_iota(jnp.int32, (1, WIDTH), 1) // SIZE
    masks = [(head_of == h) for h in range(HEADS)]

    def stacked(part):
        return jnp.concatenate([jnp.where(m, part, jnp.zeros_like(part)) for m in masks], axis=0)

    def joined(full):
        full = full.reshape(HEADS, WIN, WIDTH)
        total = jnp.where(masks[0], full[0], 0.0)
        for h in range(1, HEADS):
            total = jnp.where(masks[h], full[h], total)
        return total

    kept = []
    earth = earth_ref[...]
    group_row = lax.broadcasted_iota(jnp.int32, (1, WIN), 1) // WIN_LON
    group_col = lax.broadcasted_iota(jnp.int32, (WIN, 1), 0) // WIN_LON
    attended = []
    for w in range(2):
        rows = slice(w * WIN, (w + 1) * WIN)
        part = triple[rows]
        query, keys, vals = part[:, :WIDTH], part[:, WIDTH : 2 * WIDTH], part[:, 2 * WIDTH :]
        label_row = jnp.zeros((1, WIN), jnp.int32)
        label_col = jnp.zeros((WIN, 1), jnp.int32)
        for group in range(WIN_PL * WIN_LAT):
            label = region_ref[w * WIN_PL + group // WIN_LAT, group % WIN_LAT]
            label_row = jnp.where(group_row == group, label, label_row)
            label_col = jnp.where(group_col == group, label, label_col)
        same = label_row == label_col
        q_stack = stacked(query)
        scores = nt(q_stack, keys).reshape(HEADS, WIN, WIN) * scale + earth
        expo = jnp.where(same[None], jnp.exp(scores), 0.0)
        probs = expo / jnp.sum(expo, axis=-1, keepdims=True)
        probs_low = probs.astype(BF).reshape(HEADS * WIN, WIN)
        attended.append(joined(nn(probs_low, vals)).astype(BF))
        kept.append((q_stack, keys, vals, probs, probs_low))
    attended = jnp.concatenate(attended, axis=0)

    resid = (x + nn(attended, proj_ref[...])).astype(BF)
    normed_two, recip_two, scaled_two = layer_norm(resid.astype(F32), gain_b)
    hidden_two = scaled_two.astype(BF)
    acted, slope = gelu_parts(nn(hidden_two, up_ref[...]))
    acted_low = acted.astype(BF)
    down = tn(g_low, acted_low)
    grad_act = (nn(g_low, down_ref[...]) * slope).astype(BF)
    up = tn(hidden_two, grad_act)
    grad_hid_two = nt(grad_act, up_ref[...])
    gain_ref[...] = jnp.zeros_like(gain_ref)
    gain = jnp.sum(grad_hid_two * normed_two, axis=0, keepdims=True)
    gain_ref[2:3, :] = gain[:, :LANES]
    gain_ref[3:4, : WIDTH - LANES] = gain[:, LANES:]
    grad_resid = (
        g + norm_back(grad_hid_two, normed_two, recip_two, gain_b)
    ).astype(BF)
    wide_ref[:, 3 * WIDTH :] = tn(attended, grad_resid)
    grad_att = nt(grad_resid, proj_ref[...]).astype(BF)
    total = None
    for w in range(2):
        rows = slice(w * WIN, (w + 1) * WIN)
        q_stack, keys, vals, probs, probs_low = kept[w]
        a_stack = stacked(grad_att[rows])
        grad_prob = nt(a_stack, vals).reshape(HEADS, WIN, WIN)
        grad_score = probs * (grad_prob - jnp.sum(probs * grad_prob, axis=-1, keepdims=True))
        total = grad_score if total is None else total + grad_score
        grad_low = (grad_score * scale).astype(BF).reshape(HEADS * WIN, WIN)
        triple_ref[rows, :WIDTH] = joined(nn(grad_low, keys)).astype(BF)
        triple_ref[rows, WIDTH : 2 * WIDTH] = tn(grad_low, q_stack).astype(BF)
        triple_ref[rows, 2 * WIDTH :] = tn(probs_low, a_stack).astype(BF)
    score_ref[...] = total
    grad_triple = triple_ref[...]
    wide_ref[:, : 3 * WIDTH] = tn(hidden_one, grad_triple)
    grad_hid_one = nt(grad_triple, qkv_ref[...])
    gain = jnp.sum(grad_hid_one * normed_one, axis=0, keepdims=True)
    gain_ref[0:1, :] = gain[:, :LANES]
    gain_ref[1:2, : WIDTH - LANES] = gain[:, LANES:]
    grad = grad_resid.astype(F32) + norm_back(grad_hid_one, normed_one, recip_one, gain_a)
    grad_ref[...] = jnp.concatenate([grad[-level:], grad[:-level]], axis=0).astype(BF)
    lines = {}
    for part, whole in enumerate((wide_ref[...], up, down)):
        for k in range(6):
            lines[part * 6 + k] = whole[:, k * LANES : (k + 1) * LANES].astype(BF)
    extra = [jnp.zeros((HALF - 9 * WIDTH, LANES), BF), gain_ref[...].astype(BF)]

    def put(ref, half):
        for k in range(9):
            ref[k * WIDTH : (k + 1) * WIDTH, :] = lines[half * 9 + k]
        ref[9 * WIDTH :, :] = extra[half]

    core = core_ref[0]
    for mine in range(2):

        @pl.when(core == mine)
        def _():
            put(keep_ref, mine)
            put(send_ref, 1 - mine)


def first_sum_kernel(keep_ref, came_ref, table_ref, out_ref, total_ref, pad_ref):
    total_ref[...] = keep_ref[...].astype(F32) + came_ref[...].astype(F32)
    pad_ref[...] = jnp.zeros_like(pad_ref)
    for p in range(NEAR):
        pad_ref[p, :PIECE, :] = total_ref[p * PIECE : (p + 1) * PIECE, :]
        pad_ref[p, PIECE : PIECE + BIAS_PIECE, :] = table_ref[p * BIAS_PIECE : (p + 1) * BIAS_PIECE, :]
    out_ref[...] = pad_ref[...].astype(BF)


def second_sum_kernel(came_ref, out_ref, line_ref):
    came = came_ref[...].astype(F32)
    line_ref[:PIECE, :] = jnp.sum(came[:, :PIECE], axis=0)
    table = came[:, PIECE:].reshape(NEAR // Y // 2, Y, 2, 8, LANES)
    table = jnp.sum(jnp.sum(table, axis=2), axis=0)
    for y in range(Y):
        at = PIECE + y * BIAS_PIECE
        line_ref[at : at + BIAS_PIECE, :] = table[y, :BIAS_PIECE]
    line = line_ref[...].astype(BF)
    for n in range(FAR):
        out_ref[n] = line


def fan_kernel(came_ref, *refs):
    out_ref, line_ref, pad_ref = refs[-3:]
    line_ref[...] = jnp.sum(came_ref[...].astype(F32), axis=0)
    pad_ref[...] = jnp.zeros_like(pad_ref)
    for y in range(Y):
        at = PIECE + y * BIAS_PIECE
        pad_ref[y, :PIECE, :] = line_ref[:PIECE, :]
        pad_ref[y, PIECE : PIECE + BIAS_PIECE, :] = line_ref[at : at + BIAS_PIECE, :]
    pieces = pad_ref[...].astype(BF)
    for p in range(NEAR):
        out_ref[p] = pieces[p // 2 % Y]


def finish_kernel(
    factor, core_ref, mine_ref, came_ref, qkv_ref, proj_ref, up_ref, down_ref, gains_ref, bias_ref
):
    mine, came = mine_ref[...].astype(F32), came_ref[...].astype(F32)
    first = (jnp.zeros((1, 1, 1), jnp.int32) + core_ref[0]) == 0
    halves = [jnp.where(first, mine, came) * factor, jnp.where(first, came, mine) * factor]

    def put(block, rows, lines):
        if block >= 6:
            ref, at = (up_ref, down_ref)[block // 12], block % 6 * LANES
            ref[rows, at : at + LANES] = lines
        elif block < 4:
            qkv_ref[rows, block * LANES : (block + 1) * LANES] = lines
        elif block == 4:
            qkv_ref[rows, 4 * LANES :] = lines[:, : LANES // 2]
            proj_ref[rows, : LANES // 2] = lines[:, LANES // 2 :]
        else:
            proj_ref[rows, LANES // 2 :] = lines

    for half in range(2):
        for p in range(NEAR):
            lines = halves[half][p, :PIECE]
            at = 0
            while at < PIECE and p * PIECE + at < 9 * WIDTH:
                block, row = divmod(p * PIECE + at, WIDTH)
                count = min(PIECE - at, WIDTH - row)
                put(half * 9 + block, slice(row, row + count), lines[at : at + count])
                at += count
    p, at = divmod(9 * WIDTH, PIECE)
    gains = halves[1][p, at : at + 8]
    for n in range(2):
        gains_ref[n : n + 1, :LANES] = gains[2 * n : 2 * n + 1]
        gains_ref[n : n + 1, LANES:] = gains[2 * n + 1 : 2 * n + 2, : WIDTH - LANES]
    for p in range(NEAR):
        piece = mine[p, PIECE:]
        for r in range(BIAS_PIECE):
            h, c = divmod(p * BIAS_PIECE + r, 32)
            width = min(LANES, BIAS_POS - c * LANES)
            if width > 0:
                bias_ref[h, :, c * LANES : c * LANES + width] = piece[r : r + 1, :width]


VMEM = pl.BlockSpec(memory_space=pltpu.VMEM)
SMEM = pl.BlockSpec(memory_space=pltpu.SMEM)
ANY = pl.BlockSpec(memory_space=pl.ANY)


def kernel(function, name, outs, scratch=(), scalars=0, later=0, copies=0, flops=1_000_000, moved=1_000_000):
    shapes = tuple(jax.ShapeDtypeStruct(s, t) for s, t in outs)

    def call(*args):
        return pl.pallas_call(
            function,
            out_shape=shapes,
            in_specs=[SMEM] * scalars + [VMEM] * (len(args) - scalars - later) + [ANY] * later,
            out_specs=(VMEM,) * len(shapes),
            scratch_shapes=[pltpu.VMEM(s, t) for s, t in scratch] + [pltpu.SemaphoreType.DMA((copies,))] * (copies > 0),
            compiler_params=pltpu.CompilerParams(vmem_limit_bytes=48 * 1024 * 1024),
            cost_estimate=pl.CostEstimate(flops=flops, bytes_accessed=moved, transcendentals=0),
            name=name,
        )(*args)

    return call


QUARTER = ((2, WIN_LAT // 2, 4, WIN_LON * WIDTH // 2), BF)
cut = kernel(cut_kernel, "cut", [QUARTER] * 4, copies=8, later=2)
REST = [((WIN - LANES, 2 * LANES), jnp.int32), ((HEADS, WIN - LANES, 2 * LANES), F32)]
find_bias = kernel(
    bias_kernel,
    "find_bias",
    [((HEADS, WIN, WIN), F32), ((2, WIDTH), F32), ((4, WIN_LAT), jnp.int32)]
    + [((WIDTH, 3 * WIDTH), BF), ((WIDTH, WIDTH), BF), ((WIDTH, 4 * WIDTH), BF), ((WIDTH, 4 * WIDTH), BF)],
    REST + [((8, CHUNKS * LANES), jnp.int32)],
    copies=6,
    later=6,
    flops=20_000_000,
)
spread_bias = kernel(
    scatter_kernel,
    "spread_bias",
    [((HEADS * 32, LANES), F32)],
    REST,
    flops=1_000_000_000,
)
block_grads = kernel(
    block_kernel,
    "block_grads",
    [((CELLS, WIDTH), BF), ((HALF, LANES), BF), ((HALF, LANES), BF), ((HEADS, WIN, WIN), F32)],
    [((CELLS, 3 * WIDTH), BF), ((WIDTH, 4 * WIDTH), F32), ((HALF - 9 * WIDTH, LANES), F32)],
    scalars=2,
    flops=1_000_000_000,
    moved=4_000_000,
)
first_sum = kernel(
    first_sum_kernel, "first_sum", [((NEAR, 64, LANES), BF)], [((HALF, LANES), F32), ((NEAR, 64, LANES), F32)]
)
second_sum = kernel(
    second_sum_kernel, "second_sum", [((FAR, LINE, LANES), BF)], [((LINE, LANES), F32)]
)
fan = kernel(
    fan_kernel, "fan", [((NEAR, 64, LANES), BF)], [((LINE, LANES), F32), ((Y, 64, LANES), F32)], later=3
)


def finish(factor, core, mine, came):
    return kernel(
        lambda *refs: finish_kernel(factor, *refs),
        "finish",
        [
            ((WIDTH, 3 * WIDTH), F32),
            ((WIDTH, WIDTH), F32),
            ((WIDTH, 4 * WIDTH), F32),
            ((WIDTH, 4 * WIDTH), F32),
            ((2, WIDTH), F32),
            ((HEADS, 1, BIAS_POS), F32),
        ],
        scalars=1,
    )(core, mine, came)


def routes(lon_step, lat_step):
    lon, lat, mem = 2 * Z, 2 * Y, 2
    return [
        ((a * lat + b) * mem + c, ((a + lon_step) % lon * lat + (b + lat_step) % lat) * mem + c)
        for a in range(lon)
        for b in range(lat)
        for c in range(mem)
    ]


def shifted(own, east, south, corner):
    corner = lax.ppermute(corner, ALL, routes(-1, -1))
    east = lax.ppermute(east, ALL, routes(-1, 0))
    south = lax.ppermute(south, ALL, routes(0, -1))
    top = jnp.concatenate([own, east], axis=3)
    bottom = jnp.concatenate([south, corner], axis=3)
    return jnp.concatenate([top, bottom], axis=1).transpose(0, 2, 1, 3).reshape(2, CELLS, WIDTH)


def sent_back(grad):
    half_rows, half_cols = grad.shape[1] // 2, grad.shape[2] // 2
    east, south = grad[:, :half_rows, half_cols:], grad[:, half_rows:, :half_cols]
    corner = grad[:, half_rows:, half_cols:]
    corner = lax.ppermute(corner, ALL, routes(1, 1))
    east = lax.ppermute(east, ALL, routes(1, 0))
    south = lax.ppermute(south, ALL, routes(0, 1))
    return corner, east, south


def unshifted(grad, corner, east, south):
    own = grad[:, : grad.shape[1] // 2, : grad.shape[2] // 2]
    top = jnp.concatenate([corner, south], axis=2)
    bottom = jnp.concatenate([east, own], axis=2)
    return jnp.concatenate([top, bottom], axis=1)


def body(states, cotangent, region, pos_index, w_qkv, w_proj, w_up, w_down, gains, earth_bias):
    levels, rows, merged = states.shape[1:]
    turned = [array[0].transpose(1, 0, 2) for array in (states, cotangent)]
    quarters = cut(*[pltpu.with_memory_space_constraint(array, pltpu.HBM) for array in turned])
    far = (gains, region.T, w_qkv, w_proj, w_up, w_down.T)
    far = [pltpu.with_memory_space_constraint(array, pltpu.HBM) for array in far]
    earth, gains, region, *weights = find_bias(pos_index, earth_bias.transpose(1, 0, 2), *far)
    cells = shifted(*quarters)
    core = lax.axis_index("c").astype(jnp.int32).reshape(1)
    grad, send, keep, score = block_grads(
        region, core, cells, earth, gains, *weights
    )
    came = lax.ppermute(send, "c", SWAP)
    grad = grad.reshape(levels, rows, merged)
    back = sent_back(grad)
    (spread,) = spread_bias(pos_index, score)
    (plane,) = first_sum(keep, came, spread)
    plane = lax.all_to_all(plane, PLANE, 0, 0)
    (line,) = second_sum(plane)
    line = lax.all_to_all(line, "far", 0, 0)
    (plane,) = fan(line, *back)
    plane = lax.all_to_all(plane, PLANE, 0, 0)
    came = lax.ppermute(plane, "c", SWAP)
    factor = float(CELLS * lax.axis_size(ALL)) ** (-0.5)
    grad_qkv, grad_proj, grad_up, grad_down, grad_gains, grad_bias = finish(factor, core, plane, came)
    grad_states = unshifted(grad, *back)[None]
    return (grad_states, grad_qkv, grad_proj, grad_up, grad_down.T, grad_gains, grad_bias.transpose(1, 0, 2))


def solution(mesh):
    fine = Mesh(mesh.devices.reshape(2, FAR, 2, Y, 2, 2), ALL)
    lon, lat = ("x", "far", "pair"), ("y", "c")
    return jax.shard_map(
        body,
        mesh=fine,
        in_specs=(
            P("m", None, lat, lon),
            P("m", None, lat, lon),
            P(lat, None),
            P(),
            P(),
            P(),
            P(),
            P(),
            P(),
            P(lat, None, None),
        ),
        out_specs=(P("m", None, lat, lon), P(), P(), P(), P(), P(), P(lat, None, None)),
        check_vma=False,
    )
```
